512 devices in a mesh: dp: 16 (over z_lo, y), tensor: 32 (over x, z_hi, core).
Axes of the slice: x: 4, y: 8, z: 8 (z_hi: 4, z_lo: 2; z = z_hi * 2 + z_lo), core: 2. Of those that a mesh axis runs over, the one named last changes fastest.
Arguments:
- hidden: bfloat16 [2048, 8192], P('dp'), may hold values from -6 to 6
- target: bfloat16 [2048, 8192], P('dp'), may hold values from -15 to 15
- segments: int32 [16, 128], P('dp'), may hold values from 0 to 3, never falling along the last dimension, each value on 1 to 96 neighbouring positions
- head_map: int32 [64], P('tensor'), may hold values from 0 to 7, as said below
- decay_rate: float32 [64], P('tensor'), may hold values from 0.002 to 0.06
- dt_weight: bfloat16 [8192, 64], P('dp', 'tensor'), may hold values from -0.0625 to 0.0625
- teacher_query: bfloat16 [32, 2048, 1024], P('tensor', 'dp'), may hold values from -0.0625 to 0.0625
- teacher_key: bfloat16 [32, 2048, 128], P('tensor', 'dp'), may hold values from -0.0625 to 0.0625
- teacher_value: bfloat16 [32, 2048, 128], P('tensor', 'dp'), may hold values from -0.0625 to 0.0625
- teacher_out: bfloat16 [32, 1024, 2048], P('tensor', None, 'dp'), may hold values from -0.03125 to 0.03125
Outputs:
- layer_out: bfloat16 [2048, 8192], P('dp', 'tensor')
- grad_x: float32 [8192, 8192], P('dp', 'tensor')
- loss: float32 [], replicated
The draws below stay inside these ranges and needn't reach their ends.
Inputs may be any that keep to these rules, and one draw needn't show every extreme that they name: `head_map`: every teacher key-value head is named by exactly 8 student heads. `segments`: ids never fall along a row; the tokens of one id form one document.
All inputs are finite; a program needn't handle non-finite values.
Results may differ from the reference program's by a relative error of at most 0.034.
Values may be sent and summed in bfloat16 or wider, within the bound.
A program may use at most 64 MiB of HBM per device.

```python
import math
import jax
import jax.numpy as jnp
import numpy as np
from jax import lax

D = 8192
P_SIZE = 128
KVH = 8
HD = 2
TOK = 128
H = 64
QUART = 4
QH = 8
ROWB = 128
TOKENS = 2048
N_DP = 16
N_TENSOR = 32


def draw_head_map(key, part):
    key = jax.random.fold_in(key, 7)
    repeated = jnp.repeat(jnp.arange(KVH, dtype=jnp.int32), H // KVH)
    return jax.random.permutation(key, repeated)


def draw_target(key, part):
    key = jax.random.fold_in(key, 11)
    group = (jnp.arange(TOKENS) // TOK).astype(jnp.float32)
    frac = group / max(N_DP - 1, 1)
    scale = 1.0 + 1.5 * frac
    base = jnp.clip(jax.random.normal(key, (TOKENS, D), jnp.float32), -6.0, 6.0)
    return (base * scale[:, None]).astype(jnp.bfloat16)


def block_scale(stream_key, extent, cuts, low, top_value):
    gain, own = 1.0, jax.random.fold_in(stream_key, 6)
    for dim, blocks in cuts:
        heights = jnp.exp(jax.random.uniform(jax.random.fold_in(own, dim), (blocks,), jnp.float32, low / len(cuts), top_value / len(cuts)))
        gain = gain * jnp.repeat(heights, extent[dim] // blocks).reshape([-1 if axis == dim else 1 for axis in range(len(extent))])
    return gain


def profile(number_of, total, most, lean):
    weights = [(1 << 20) // math.isqrt(grade ** lean) + 1 for grade in range(2, number_of + 1)]
    rest, holding = total - most - (number_of - 1), [1] * (number_of - 1)
    while rest > 0:
        free = [i for i in range(number_of - 1) if holding[i] < most]
        mass, remaining = sum([weights[i] for i in free]), rest
        for i in free:
            addition = min(most - holding[i], max(1, remaining * weights[i] // mass), rest)
            holding[i] = holding[i] + addition
            rest = rest - addition
    return np.array([most] + holding)


def uneven_parts(stream_key, number_of, total, reach, lean):
    if number_of == 2:
        one = jax.random.randint(stream_key, (), max(1, total - reach), min(reach, total - 1) + 1)
        return jnp.stack([one, total - one])
    tallies = jnp.asarray(profile(number_of, total, reach, lean), jnp.int32)
    twos = (number_of - 1) // 2
    donor, taker = tallies[1:1 + 2 * twos:2], tallies[2:2 + 2 * twos:2]
    slack = jnp.minimum(donor - 1, reach - taker)
    shifted = jax.random.randint(jax.random.fold_in(stream_key, 1), (twos,), 0, 1 << 20) % (slack + 1)
    tallies = tallies.at[1:1 + 2 * twos:2].set(donor - shifted).at[2:2 + 2 * twos:2].set(taker + shifted)
    return tallies[jax.random.permutation(jax.random.fold_in(stream_key, 2), number_of)]


def gaussian(key, extent, deviation, limit, cuts=(), held_as=jnp.bfloat16):
    level = block_scale(key, extent, cuts, -0.22, 0.18) if cuts else 1.0
    array = jax.random.normal(key, extent, jnp.float32) * deviation * level
    return jnp.minimum(jnp.maximum(array, -limit), limit).astype(held_as)


def setup_inputs(seed: int = 0) -> dict:
    key_list = jax.random.split(jax.random.key(seed), 11)
    return {
        "hidden": gaussian(key_list[0], (TOKENS, D), 1.0, 6.0, ((0, 16),)),
        "target": draw_target(jax.random.fold_in(key_list[10], 71), 0),
        "segments": jax.vmap(lambda own: jnp.searchsorted(jnp.cumsum(uneven_parts(own, max(2, TOK // 32), TOK, 3 * TOK // 4, 0)), jnp.arange(TOK), side="right"))(jax.random.split(key_list[2], N_DP)).reshape((N_DP, TOK)).astype(jnp.int32),
        "head_map": draw_head_map(jax.random.fold_in(key_list[10], 71), 0),
        "decay_rate": jnp.clip(jnp.exp(math.log(0.06) - 3.4011973 * jax.random.uniform(key_list[4], (H,), jnp.float32) ** block_scale(key_list[4], (H,), ((0, 32),), -0.2, 0.2)), 0.002, 0.06),
        "dt_weight": gaussian(key_list[5], (D, H), D ** -0.5, 0.0625, ((0, 16), (1, 32))),
        "teacher_query": gaussian(key_list[6], (N_TENSOR, D // QUART, QH * P_SIZE), D ** -0.5, 0.0625, ((0, 32), (1, 16))),
        "teacher_key": gaussian(key_list[7], (N_TENSOR, D // QUART, P_SIZE), D ** -0.5, 0.0625, ((0, 32), (1, 16))),
        "teacher_value": gaussian(key_list[8], (N_TENSOR, D // QUART, P_SIZE), D ** -0.5, 0.0625, ((0, 32), (1, 16))),
        "teacher_out": gaussian(key_list[9], (N_TENSOR, QH * P_SIZE, D // QUART), (4 * H * P_SIZE) ** -0.5, 0.03125, ((0, 32), (2, 16))),
    }


def teacher_rows(stacked):
    columns = stacked.shape[2]
    parts = stacked.reshape(KVH, QUART, N_DP, ROWB, columns)
    return parts.transpose(2, 1, 3, 0, 4).reshape(D, KVH * columns)


def teacher_columns(stacked):
    parts = stacked.reshape(KVH, QUART, QH * P_SIZE, N_DP, ROWB)
    return parts.transpose(0, 2, 3, 1, 4).reshape(H * P_SIZE, D)


def mixing_of(c_group, b_group, dt_group, rates, seg_row):
    cumulated = jnp.cumsum(rates[None, :] * dt_group, axis=0)
    positions = jnp.arange(TOK)
    visible = (seg_row[:, None] == seg_row[None, :]) & (positions[None, :] <= positions[:, None])
    distance = cumulated.T[:, :, None] - cumulated.T[:, None, :]
    distance = jnp.where(visible[None], distance, 0.0)
    decays = jnp.where(visible[None], jnp.exp(-distance), 0.0)
    scores = jnp.einsum("thp,jhp->htj", c_group.astype(jnp.float32), b_group.astype(jnp.float32), precision=lax.Precision.HIGHEST)
    return scores * decays


def reference(hidden, target, segments, head_map, decay_rate, dt_weight, teacher_query, teacher_key, teacher_value, teacher_out):
    w_query = teacher_rows(teacher_query)
    w_key = teacher_rows(teacher_key).reshape(D, KVH, P_SIZE)
    w_value = teacher_rows(teacher_value).reshape(D, KVH, P_SIZE)
    w_out = teacher_columns(teacher_out)
    w_b = w_key[:, head_map, :].reshape(D, H * P_SIZE)
    w_x = w_value[:, head_map, :].reshape(D, H * P_SIZE)
    c_proj = (jnp.dot(hidden, w_query, preferred_element_type=jnp.float32) * (P_SIZE ** -0.5)).astype(jnp.bfloat16)
    b_proj = jnp.dot(hidden, w_b, preferred_element_type=jnp.float32).astype(jnp.bfloat16)
    x_proj = jnp.dot(hidden, w_x, preferred_element_type=jnp.float32).astype(jnp.bfloat16)
    step_sizes = jax.nn.softplus(jnp.dot(hidden, dt_weight, preferred_element_type=jnp.float32))
    shape_four = (N_DP, TOK, H, P_SIZE)
    c_four = c_proj.reshape(shape_four)
    b_four = b_proj.reshape(shape_four)
    x_four = x_proj.reshape(shape_four)
    dt_three = step_sizes.reshape(N_DP, TOK, H)

    def forward_group(items):
        c_group, b_group, x_group, dt_group, seg_row = items
        mixing = mixing_of(c_group, b_group, dt_group, decay_rate, seg_row)
        source = dt_group[:, :, None] * x_group.astype(jnp.float32)
        return jnp.einsum("htj,jhp->thp", mixing, source, precision=lax.Precision.HIGHEST).astype(jnp.bfloat16)

    mixed = lax.map(forward_group, (c_four, b_four, x_four, dt_three, segments))
    mixed_blocks = mixed.reshape(TOKENS, H // HD, HD * P_SIZE).transpose(1, 0, 2)
    out_blocks = w_out.reshape(H // HD, HD * P_SIZE, D)

    def add_block(running, items):
        block_rows, block_weight = items
        term = jnp.dot(block_rows, block_weight, preferred_element_type=jnp.float32).astype(jnp.bfloat16)
        term = lax.optimization_barrier(term)
        return running + term.astype(jnp.float32), None

    summed, _ = lax.scan(add_block, jnp.zeros((TOKENS, D), jnp.float32), (mixed_blocks, out_blocks))
    layer_out = summed.astype(jnp.bfloat16)
    residual = layer_out.astype(jnp.float32) - target.astype(jnp.float32)
    loss = jnp.sum(residual * residual) / (TOKENS * D)
    grad_out = (2.0 * residual / TOKENS).astype(jnp.bfloat16)
    grad_heads = jnp.dot(grad_out, w_out.T, preferred_element_type=jnp.float32).astype(jnp.bfloat16)

    def backward_group(items):
        c_group, b_group, dt_group, seg_row, dy_group = items
        mixing = mixing_of(c_group, b_group, dt_group, decay_rate, seg_row)
        back = jnp.einsum("htj,thp->jhp", mixing, dy_group.astype(jnp.float32), precision=lax.Precision.HIGHEST)
        return (dt_group[:, :, None] * back).astype(jnp.bfloat16)

    grad_source = lax.map(backward_group, (c_four, b_four, dt_three, segments, grad_heads.reshape(shape_four)))
    hidden_groups = hidden.reshape(N_DP, TOK, D)
    source_groups = grad_source.reshape(N_DP, TOK, H * P_SIZE)

    def add_group(running, items):
        group_rows, group_grads = items
        term = lax.dot_general(group_rows, group_grads, (((0,), (0,)), ((), ())), preferred_element_type=jnp.float32).astype(jnp.bfloat16)
        term = lax.optimization_barrier(term)
        return running + term.astype(jnp.float32), None

    grad_x, _ = lax.scan(add_group, jnp.zeros((D, H * P_SIZE), jnp.float32), (hidden_groups, source_groups))
    return layer_out, grad_x, loss
```

```python
import jax
import jax.numpy as jnp
from jax import lax
from jax.experimental import pallas as pl
from jax.experimental.pallas import tpu as pltpu
from jax.sharding import PartitionSpec as P

F32 = jnp.float32
BF16 = jnp.bfloat16
MESH = pl.DeviceIdType.MESH
TOK = 128
TOKENS = 2048
WIDTH = 8192
NY = 8
N_SEM = 192


def dot(a, b, **kw):
    return jnp.dot(a, b, preferred_element_type=F32, **kw)


def dot_t(a, b, **kw):
    return lax.dot_general(a, b, (((1,), (1,)), ((), ())), preferred_element_type=F32, **kw)


def kernel(
    hid_any, tgt_any, seg_ref, map_ref, rate_ref, dtw_ref, q_any, k_any, v_any, o_any,
    lo_ref, gx_ref, loss_ref,
    hid, tg, qg, kvg, og, dtb, hx, hs, ht, hg,
    kvacc, kvp, kvr1, kvt, kvs, kvr2, kvall,
    cacc, cp1, cr1, cp2, cr2,
    w2, mix, dtc, yb, ycat,
    lacc, lp, lr1, lt, ls, lr2, lob,
    gob, dacc, dp1, dr1, dp2, dr2, dxb,
    lsa, lsb, lsb1, lsc, lsc2, lring,
    ssem, rsem, lsem,
):
    dp = lax.axis_index("dp")
    tn = lax.axis_index("tensor")
    zl, y = lax.div(dp, 8), lax.rem(dp, 8)
    x, zh, c = lax.div(tn, 8), lax.rem(lax.div(tn, 2), 4), lax.rem(tn, 2)
    zh1, zh0 = lax.div(zh, 2), lax.rem(zh, 2)
    s, q = lax.div(tn, 4), lax.rem(tn, 4)

    def dev(zl_=zl, y_=y, x_=x, zh1_=zh1, zh0_=zh0, c_=c):
        return (zl_ * 8 + y_, x_ * 8 + zh1_ * 4 + zh0_ * 2 + c_)

    def s_dev(s_):
        return dev(x_=lax.div(s_, 2), zh1_=lax.rem(s_, 2))

    flip_zl, flip_c, flip_h = dev(zl_=1 - zl), dev(c_=1 - c), dev(zh0_=1 - zh0)
    flip_zh = dev(zl_=1 - zl, zh0_=1 - zh0)
    flip_h1 = dev(zh1_=1 - zh1)
    line = (flip_h, flip_zl, flip_zh)

    count = [0]
    pending = []

    def sems(n=1):
        first = count[0]
        count[0] += n
        return first

    def rcopy(src, dst, i, target):
        return pltpu.make_async_remote_copy(
            src_ref=src, dst_ref=dst, send_sem=ssem.at[i], recv_sem=rsem.at[i],
            device_id=target, device_id_type=MESH,
        )

    def send(src, dst, i, target):
        copy = rcopy(src, dst, i, target)
        copy.start()
        pending.append(copy)

    def arrived(dst, i):
        rcopy(dst, dst, i, flip_c).wait_recv()

    def column(index):
        return pl.ds(pl.multiple_of(index * 128, 128), 128)

    def stage(src, dst, i):
        copy = pltpu.make_async_copy(src, dst, lsem.at[i])
        copy.start()
        return copy

    hid_in = stage(hid_any, hid, 0)
    key_in = stage(k_any, kvg.at[y, :, pl.ds(0, 128)], 1)
    value_in = stage(v_any, kvg.at[y, :, pl.ds(128, 128)], 2)
    query_in = stage(q_any, qg.at[y], 3)
    out_in = stage(o_any, og.at[y], 4)
    own_target = tgt_any.at[:, column((zl * 8 + s) * 4 + q)]
    target_in = stage(own_target, tg.at[zl], 5)

    lo_t = lax.div(tn, 16)
    lo_s = lax.div(lax.rem(tn, 16), 2)
    lo_q = 2 * lax.rem(tn, 2)

    def lo_source(slot):
        return (lo_t * 8 + y, lo_s * 4 + lo_q + slot)

    perm_from = (lax.rem(lax.div(tn, 2) + 8, 16), 2 * dp + c)
    perm_to = (lax.div(tn, 2), 2 * lax.rem(dp + 8, 16) + c)
    greeted = [dev(y_=lax.rem(y + 1, 8)), dev(y_=lax.rem(y + 7, 8))]
    greeted += [flip_zl, flip_c, flip_h, flip_zh]
    greeted += [s_dev(lax.rem(s + d, 8)) for d in range(1, 8)]

    def zh_dev(d):
        other = lax.rem(zh + d, 4)
        return dev(zh1_=lax.div(other, 2), zh0_=lax.rem(other, 2))

    def x_dev(d):
        return dev(x_=lax.rem(x + d, 4))

    greeted += [zh_dev(d) for d in range(1, 4)]
    greeted += [perm_from, lo_source(0), lo_source(1)]
    barrier = pltpu.get_barrier_semaphore()
    for target in greeted:
        pl.semaphore_signal(barrier, inc=1, device_id=target, device_id_type=MESH)

    dtb[y, pl.ds(pl.multiple_of(zl * 8, 8), 8), :] = dtw_ref[...]
    hid_in.wait()
    for i in range(NY):
        hx[zl, i] = hid[:, column((zl * 8 + i) * 4 + q)]
        hs[i] = hid[:, column(((1 - zl) * 8 + i) * 4 + q)]
    tile = hid[:, pl.ds(pl.multiple_of(tn * 256, 256), 256)]
    ht[...] = tile.astype(F32).T.astype(BF16)
    key_in.wait()
    value_in.wait()
    pl.semaphore_wait(barrier, len(greeted))

    class Ring:
        def __init__(self, part, chunks):
            self.part, self.chunks = part, chunks
            self.base = sems(8 * chunks)

        def live(self, k, d, ch):
            if k < 3:
                return True
            return d == 0 if self.chunks == 1 else d == ch

        def block(self, k, d):
            return lax.rem(y + (8 - k if d == 0 else k), 8)

        def sem(self, k, d, ch):
            return self.base + (k * 2 + d) * self.chunks + ch

        def send(self, k, d, ch):
            ref = self.part(self.block(k, d), ch)
            to = dev(y_=lax.rem(y + (1 if d == 0 else 7), 8))
            send(ref, ref, self.sem(k, d, ch), to)

        def start(self, chunks=None):
            for ch in range(self.chunks):
                for d in range(2):
                    self.send(0, d, ch)

        def step(self, k):
            for ch in range(self.chunks):
                for d in range(2):
                    if self.live(k, d, ch):
                        arrived(self.part(self.block(k + 1, d), ch), self.sem(k, d, ch))
                        if k < 3 and self.live(k + 1, d, ch):
                            self.send(k + 1, d, ch)

    kv_ring = Ring(lambda b, ch: kvg.at[b, pl.ds(ch * 64, 64)], 2)
    q_ring = Ring(lambda b, ch: qg.at[b, pl.ds(ch * 64, 64)], 2)
    o_ring = Ring(lambda b, ch: og.at[b, pl.ds(ch * 512, 512)], 2)
    dt_ring = Ring(lambda b, ch: dtb.at[b, pl.ds(ch * 8, 8)], 2)
    dx_ring = Ring(lambda b, ch: dxb.at[b, ch], 2)
    loss_ring = Ring(lambda b, ch: lring.at[b], 1)

    h_sem, t_sem, dt_sem, p_sem = sems(), sems(), sems(), sems()
    kv_ring.start()
    send(hs, hx.at[zl], h_sem, flip_zl)
    dt_own = dtb.at[y, pl.ds(pl.multiple_of(zl * 8, 8), 8)]
    send(dt_own, dt_own, dt_sem, flip_zl)
    send(ht, hg.at[c, lax.rem(dp + 8, 16)], p_sem, perm_to)
    query_in.wait()
    kv_ring.step(0)
    q_ring.start()
    other_target = tgt_any.at[:, column(((1 - zl) * 8 + s) * 4 + q)]
    send(other_target, tg.at[zl], t_sem, flip_zl)
    kv_ring.step(1)

    def rows_of(i):
        return jnp.concatenate([hx[0, i], hx[1, i]], axis=0)

    kvacc[...] = jnp.zeros_like(kvacc)
    cacc[...] = jnp.zeros_like(cacc)
    dacc[...] = jnp.zeros_like(dacc)
    arrived(hx.at[1 - zl], h_sem)
    kv_ring.step(2)
    arrived(hg.at[c, lax.div(tn, 2)], p_sem)
    hz_sem = sems(3)
    own_tile = hg.at[c, lax.div(tn, 2)]
    for d in range(1, 4):
        send(own_tile, own_tile, hz_sem + d - 1, zh_dev(d))
    arrived(dtb.at[y, pl.ds(pl.multiple_of((1 - zl) * 8, 8), 8)], dt_sem)
    dt_ring.start()
    kv_ring.step(3)

    def kv_step(i, carry):
        kvacc[...] += dot(rows_of(i), kvg[i])
        return carry

    lax.fori_loop(0, NY, kv_step, 0)
    k1_sem, k2_sem, k3_sem, k4_sem = sems(), sems(3), sems(7), sems()
    for zz in range(2):
        kvp[zz] = kvacc[pl.ds(pl.multiple_of(zz * 128 + (1 - c) * 64, 64), 64), :].astype(BF16)
    send(kvp, kvr1, k1_sem, flip_c)
    q_ring.step(0)
    dt_ring.step(0)
    arrived(kvr1, k1_sem)
    for zz in range(2):
        part = kvacc[pl.ds(pl.multiple_of(zz * 128 + c * 64, 64), 64), :] + kvr1[zz].astype(F32)
        kvt[zz] = part
        kvs[zz] = part.astype(BF16)
    send(kvs.at[zl], kvr2.at[0], k2_sem, flip_h)
    send(kvs.at[1 - zl], kvr2.at[1], k2_sem + 1, flip_zl)
    send(kvs.at[1 - zl], kvr2.at[2], k2_sem + 2, flip_zh)

    def q_block(i):
        rows = rows_of(i)
        for j in range(4):
            cacc[j] += dot(rows, qg[i, :, pl.ds(j * 256, 256)])

    def q_pair(k):
        def body(i, carry):
            q_block(lax.rem(y + jnp.where(i == 0, k, 8 - k), 8))
            return carry
        lax.fori_loop(0, 2, body, 0)

    q_block(y)
    hx_sem = sems(3)
    for d in range(1, 4):
        arrived(hg.at[c, x * 4 + lax.rem(zh + 4 - d, 4)], hz_sem + d - 1)
    quad = hg.at[c, pl.ds(x * 4, 4)]
    for d in range(1, 4):
        send(quad, quad, hx_sem + d - 1, x_dev(d))
    dt_ring.step(1)
    q_ring.step(1)
    for j in range(3):
        arrived(kvr2.at[j], k2_sem + j)
    kvall[c, s] = (
        kvt[zl] + kvr2[0].astype(F32) + kvr2[1].astype(F32) + kvr2[2].astype(F32)
    ).astype(BF16)
    own_kv = kvall.at[c, s]
    for d in range(1, 8):
        send(own_kv, own_kv, k3_sem + d - 1, s_dev(lax.rem(s + d, 8)))
    q_pair(1)
    dt_ring.step(2)
    out_in.wait()
    o_ring.start()
    q_ring.step(2)
    q_pair(2)
    dt_ring.step(3)
    for d in range(1, 8):
        arrived(kvall.at[c, lax.rem(s + 8 - d, 8)], k3_sem + d - 1)
    send(kvall.at[c], kvall.at[c], k4_sem, flip_c)

    w2[...] = jnp.zeros_like(w2)
    for m in range(16):
        for j in range(4):
            for h in range(2):
                w2[h:h + 1, pl.ds((m * 4 + j) * 128, 128)] = dtb[
                    m % 8, pl.ds((m // 8) * 8 + h * 4 + j, 1), :
                ]
    q_ring.step(3)
    lax.fori_loop(3, 5, lambda i, carry: (q_block(lax.rem(y + i, 8)), carry)[1], 0)
    q_block(lax.rem(y + 5, 8))

    class Sum8:
        def __init__(self, acc, p1, r1, p2, r2):
            self.acc, self.p1, self.r1, self.p2, self.r2 = acc, p1, r1, p2, r2
            self.s1, self.s2 = sems(), sems(3)

        def first(self):
            for zz in range(2):
                for hh in range(2):
                    self.p1[zz, hh] = self.acc[hh * 2 + 1 - c, pl.ds(zz * 128, 128), :].astype(BF16)
            send(self.p1, self.r1, self.s1, flip_c)

        def second(self):
            arrived(self.r1, self.s1)
            for zz in range(2):
                for hh in range(2):
                    rows = pl.ds(zz * 128, 128)
                    part = self.acc[hh * 2 + c, rows, :] + self.r1[zz, hh].astype(F32)
                    self.acc[hh * 2 + c, rows, :] = part
                    self.p2[zz, hh] = part.astype(BF16)
            send(self.p2.at[1 - zl, 1 - zh0], self.r2.at[2], self.s2 + 2, flip_zh)
            send(self.p2.at[zl, 1 - zh0], self.r2.at[0], self.s2, flip_h)
            send(self.p2.at[1 - zl, zh0], self.r2.at[1], self.s2 + 1, flip_zl)

        def third(self):
            for j in range(3):
                arrived(self.r2.at[j], self.s2 + j)
            own = self.acc[zh0 * 2 + c, pl.ds(pl.multiple_of(zl * 128, 128), 128), :]
            return own + self.r2[0].astype(F32) + self.r2[1].astype(F32) + self.r2[2].astype(F32)

    c_sum = Sum8(cacc, cp1, cr1, cp2, cr2)
    d_sum = Sum8(dacc, dp1, dr1, dp2, dr2)
    c_sum.first()
    o_ring.step(0)
    c_sum.second()

    best = dict(precision=lax.Precision.HIGHEST)
    weights = w2[...].astype(BF16)

    def softplus(v):
        return jnp.maximum(v, 0.0) + jnp.log1p(jnp.exp(-jnp.abs(v)))

    step_col = softplus(dot_t(hid[...], weights))
    step_row = softplus(dot_t(weights, hid[...]))
    dtc[...] = step_col
    rate0, rate1 = rate_ref[0], rate_ref[1]
    n_lane = step_col.shape[1]
    lane = lax.broadcasted_iota(jnp.int32, (TOK, n_lane), 1)
    subl = lax.broadcasted_iota(jnp.int32, (n_lane, TOK), 0)
    at_t = lax.broadcasted_iota(jnp.int32, (TOK, TOK), 0)
    at_j = lax.broadcasted_iota(jnp.int32, (TOK, TOK), 1)
    lower = (at_j <= at_t).astype(F32)
    upper = (at_t <= at_j).astype(F32)
    cs_col = dot(lower, step_col * jnp.where(lane == 0, rate0, rate1), **best)
    cs_row = dot(step_row * jnp.where(subl == 0, rate0, rate1), upper, **best)
    seg_row = jnp.broadcast_to(seg_ref[...].astype(F32), (TOK, TOK))
    visible = (seg_row == seg_row.T) & (at_j <= at_t)
    for h in range(2):
        distance = jnp.where(visible, cs_col[:, h:h + 1] - cs_row[h:h + 1, :], 0.0)
        mix[h] = jnp.where(visible, jnp.exp(-distance), 0.0)

    o_ring.step(1)
    arrived(kvall.at[1 - c], k4_sem)
    y_sem, y2_sem = sems(3), sems()
    c_full = (c_sum.third() * (128 ** -0.5)).astype(BF16)
    for h in range(2):
        head = map_ref[h]
        both = jnp.concatenate([kvall[0, head], kvall[1, head]], axis=0)
        scores = dot_t(c_full[:, h * 128:(h + 1) * 128], both[:, :128])
        mixing = scores * mix[h]
        mix[h] = mixing
        source = dtc[:, h:h + 1] * both[:, 128:].astype(F32)
        yb[c, zl, zh0, :, pl.ds(h * 128, 128)] = dot(mixing, source, **best).astype(BF16)
    own_y = yb.at[c, zl, zh0]
    send(own_y, own_y, y_sem + 2, flip_zh)
    send(own_y, own_y, y_sem, flip_h)
    send(own_y, own_y, y_sem + 1, flip_zl)
    o_ring.step(2)
    arrived(yb.at[c, zl, 1 - zh0], y_sem)
    arrived(yb.at[c, 1 - zl, zh0], y_sem + 1)
    arrived(yb.at[c, 1 - zl, 1 - zh0], y_sem + 2)
    send(yb.at[c], yb.at[c], y2_sem, flip_c)
    hc_sem = sems()
    for d in range(1, 4):
        arrived(hg.at[c, pl.ds(lax.rem(x + 4 - d, 4) * 4, 4)], hx_sem + d - 1)
    o_ring.step(3)
    arrived(yb.at[1 - c], y2_sem)
    send(hg.at[c], hg.at[c], hc_sem, flip_c)
    for zz in range(2):
        for hh in range(2):
            for cc in range(2):
                ycat[pl.ds(zz * 128, 128), pl.ds((hh * 2 + cc) * 256, 256)] = yb[cc, zz, hh]

    l1_sem, l2_sem = sems(3), sems()
    for d in (1, 2, 3, 0):
        at = lax.rem(x + d, 4)

        def l_block(j, carry):
            value = dot(ycat[...], og[at * 2 + j])
            lacc[at * 2 + j] = value
            lp[at * 2 + j] = value.astype(BF16)
            return carry

        lax.fori_loop(0, 2, l_block, 0)
        if d:
            send(lp.at[pl.ds(at * 2, 2)], lr1.at[d - 1], l1_sem + d - 1, x_dev(d))
    for d in range(3):
        arrived(lr1.at[d], l1_sem + d)
    for j in range(2):
        lt[j] = (
            lacc[x * 2 + j]
            + lr1[0, j].astype(F32) + lr1[1, j].astype(F32) + lr1[2, j].astype(F32)
        )
    ls[...] = lt[1 - zh1].astype(BF16)
    send(ls, lr2, l2_sem, flip_h1)
    target_in.wait()
    arrived(tg.at[1 - zl], t_sem)
    arrived(lr2, l2_sem)
    layer = (lt[zh1] + lr2[...].astype(F32)).astype(BF16)
    g1_sem, g2_sem, la_sem, la2_sem = sems(), sems(3), sems(), sems(3)
    squares = jnp.zeros((8, 128), F32)
    for zz in range(2):
        rows = layer[zz * 128:(zz + 1) * 128]
        lob[zz] = rows
        residual = rows.astype(F32) - tg[zz].astype(F32)
        gob[s, zz] = (2.0 * residual / TOKENS).astype(BF16)
        squares += jnp.sum((residual * residual).reshape(16, 8, 128), axis=0)
    lsa[s] = squares
    send(gob.at[s], gob.at[s], g1_sem, flip_h1)
    send(lsa.at[s], lsa.at[s], la_sem, flip_h1)
    arrived(gob.at[2 * x + 1 - zh1], g1_sem)
    pair = gob.at[pl.ds(x * 2, 2)]
    for d in (2, 1, 3):
        send(pair, pair, g2_sem + d - 1, x_dev(d))
    arrived(lsa.at[2 * x + 1 - zh1], la_sem)
    loss_pair = lsa.at[pl.ds(x * 2, 2)]
    for d in range(1, 4):
        send(loss_pair, loss_pair, la2_sem + d - 1, x_dev(d))

    lo_sem = sems(2)
    lo_tn = 16 * zl + 2 * s + lax.div(q, 2)
    slot = lax.rem(q, 2)
    lo_dst = lo_ref.at[:, column(slot)]
    lo_copies = []
    for zz in range(2):
        to = (zz * 8 + y, lo_tn)
        here = (zl == zz) & (lo_tn == tn)
        copy = pltpu.make_async_remote_copy(
            src_ref=lob.at[zz], dst_ref=lo_dst, send_sem=ssem.at[lo_sem + zz],
            recv_sem=rsem.at[lo_sem + slot], device_id=to, device_id_type=MESH,
        )
        lo_copies.append((copy, here))

        @pl.when(here)
        def _():
            lo_ref[:, column(slot)] = lob[zz]

        @pl.when(jnp.logical_not(here))
        def _():
            copy.start()

    def d_pair(at):
        def body(j, carry):
            i = at * 2 + j
            rows = jnp.concatenate([gob[i, 0], gob[i, 1]], axis=0)
            for k in range(4):
                dacc[k] += dot_t(rows, og[i, pl.ds(k * 256, 256), :])
            return carry
        lax.fori_loop(0, 2, body, 0)

    d_pair(x)
    for d in range(1, 4):
        at = lax.rem(x + 4 - d, 4)
        arrived(gob.at[pl.ds(at * 2, 2)], g2_sem + d - 1)
        d_pair(at)
    d_sum.first()
    lb_sem, lc_sem = sems(), sems(3)
    for d in range(1, 4):
        arrived(lsa.at[pl.ds(lax.rem(x + 4 - d, 4) * 2, 2)], la2_sem + d - 1)
    total = lsa[0]
    for i in range(1, 8):
        total += lsa[i]
    lsb[...] = total
    send(lsb, lsb1, lb_sem, flip_c)
    d_sum.second()
    arrived(lsb1, lb_sem)
    lsc[...] = lsb[...] + lsb1[...]
    for j in range(3):
        send(lsc, lsc2.at[j], lc_sem + j, line[j])
    dy = d_sum.third().astype(BF16).astype(F32)
    dx_sem = sems()
    for h in range(2):
        back = dot(mix[h].T, dy[:, h * 128:(h + 1) * 128], **best)
        dxb[y, zl, :, pl.ds(h * 128, 128)] = (dtc[:, h:h + 1] * back).astype(BF16)
    send(dxb.at[y, zl], dxb.at[y, zl], dx_sem, flip_zl)
    for j in range(3):
        arrived(lsc2.at[j], lc_sem + j)
    lring[y] = lsc[...] + lsc2[0] + lsc2[1] + lsc2[2]
    arrived(dxb.at[y, 1 - zl], dx_sem)
    dx_ring.start()
    loss_ring.start()
    arrived(hg.at[1 - c], hc_sem)

    def g_block(i, first=False):
        grads = jnp.concatenate([dxb[i, 0], dxb[i, 1]], axis=0)
        for b in range(2):
            tokens = jnp.concatenate([hg[b, 8 + i], hg[b, i]], axis=1)
            rows = pl.ds(b * 256, 256)
            if first:
                gx_ref[rows, :] = dot(tokens, grads)
            else:
                gx_ref[rows, :] += dot(tokens, grads)

    g_block(y, True)
    for k in range(4):
        dx_ring.step(k)
        loss_ring.step(k)
        g_block(lax.rem(y + 7 - k, 8))
        if k < 3:
            g_block(lax.rem(y + k + 1, 8))
    total = jnp.sum(jnp.sum(lring[...], axis=0), axis=0, keepdims=True)
    total = jnp.sum(total, axis=1, keepdims=True) / (TOKENS * WIDTH)
    loss_ref[...] = jnp.broadcast_to(total, (8, 128))

    for copy in pending:
        copy.wait_send()
    for copy, here in lo_copies:
        @pl.when(jnp.logical_not(here))
        def _():
            copy.wait_send()
    for k in range(2):
        from_dp, from_tn = lo_source(k)
        here = (from_dp == dp) & (from_tn == tn)

        @pl.when(jnp.logical_not(here))
        def _():
            arrived(lo_ref.at[:, pl.ds(k * 128, 128)], lo_sem + k)


def local(
    hidden, target, segments, head_map, decay_rate, dt_weight,
    teacher_query, teacher_key, teacher_value, teacher_out,
):
    steps = dt_weight.astype(F32).T.reshape(8, 128)
    anywhere = pl.BlockSpec(memory_space=pl.ANY)
    vmem = pl.BlockSpec(memory_space=pltpu.VMEM)
    smem = pl.BlockSpec(memory_space=pltpu.SMEM)

    def b(*shape):
        return pltpu.VMEM(shape, BF16)

    def f(*shape):
        return pltpu.VMEM(shape, F32)

    scratch = [
        b(128, 8192), b(2, 128, 128), b(8, 128, 1024), b(8, 128, 256), b(8, 1024, 128),
        f(8, 16, 128), b(2, 8, 128, 128), b(8, 128, 128), b(256, 128), b(2, 16, 256, 128),
        f(256, 256), b(2, 64, 256), b(2, 64, 256), f(2, 64, 256), b(2, 64, 256), b(3, 64, 256),
        b(2, 8, 64, 256),
        f(4, 256, 256), b(2, 2, 128, 256), b(2, 2, 128, 256), b(2, 2, 128, 256), b(3, 128, 256),
        f(16, 8192), f(2, 128, 128), f(128, 16), b(2, 2, 2, 128, 256), b(256, 1024),
        f(8, 256, 128), b(8, 256, 128), b(3, 2, 256, 128), f(2, 256, 128), b(256, 128),
        b(256, 128), b(2, 128, 128),
        b(8, 2, 128, 128), f(4, 256, 256), b(2, 2, 128, 256), b(2, 2, 128, 256),
        b(2, 2, 128, 256), b(3, 128, 256), b(8, 2, 128, 256),
        f(8, 8, 128), f(8, 128), f(8, 128), f(8, 128), f(3, 8, 128), f(8, 8, 128),
        pltpu.SemaphoreType.DMA((N_SEM,)), pltpu.SemaphoreType.DMA((N_SEM,)),
        pltpu.SemaphoreType.DMA((6,)),
    ]
    layer_out, grad_x, loss = pl.pallas_call(
        kernel,
        out_shape=(
            jax.ShapeDtypeStruct((128, 256), BF16),
            jax.ShapeDtypeStruct((512, 256), F32),
            jax.ShapeDtypeStruct((8, 128), F32),
        ),
        in_specs=[anywhere, anywhere, vmem, smem, smem, vmem] + [anywhere] * 4,
        out_specs=(vmem, vmem, vmem),
        scratch_shapes=scratch,
        compiler_params=pltpu.CompilerParams(
            collective_id=0, has_side_effects=True, vmem_limit_bytes=48 * 1024 * 1024
        ),
    )(
        hidden, target, segments, head_map, decay_rate, steps,
        teacher_query[0], teacher_key[0], teacher_value[0], teacher_out[0],
    )
    return layer_out, grad_x, loss[0, 0]


def solution(mesh):
    in_specs = (
        P("dp", None),
        P("dp", None),
        P("dp", None),
        P("tensor"),
        P("tensor"),
        P("dp", "tensor"),
        P("tensor", "dp", None),
        P("tensor", "dp", None),
        P("tensor", "dp", None),
        P("tensor", None, "dp"),
    )
    out_specs = (P("dp", "tensor"), P("dp", "tensor"), P())
    return jax.shard_map(local, mesh=mesh, in_specs=in_specs, out_specs=out_specs, check_vma=False)
```

```python
import jax
import jax.numpy as jnp
from jax import lax
from jax.experimental import pallas as pl
from jax.experimental.pallas import tpu as pltpu
from jax.sharding import PartitionSpec as P

F32 = jnp.float32
BF16 = jnp.bfloat16
MESH = pl.DeviceIdType.MESH
TOK = 128
TOKENS = 2048
WIDTH = 8192
NY = 8
N_SEM = 192


def dot(a, b, **kw):
    return jnp.dot(a, b, preferred_element_type=F32, **kw)


def dot_t(a, b, **kw):
    return lax.dot_general(a, b, (((1,), (1,)), ((), ())), preferred_element_type=F32, **kw)


def kernel(
    hid_any, tgt_any, seg_ref, map_ref, rate_ref, dtw_ref, q_any, k_any, v_any, o_any,
    lo_ref, gx_ref, loss_ref,
    hid, tg, qg, kvg, og, dtb, hx, hs, ht, hg,
    kvacc, kvp, kvr1, kvt, kvs, kvr2, kvall,
    cacc, cp1, cr1, cp2, cr2,
    w2, mix, dtc, yb, ycat,
    lp, lr1, lt, ls, lr2, lob,
    gob, dacc, dp1, dr1, dp2, dr2, dxb,
    lsa, lsb, lsb1, lsc, lsc2, lring,
    ssem, rsem, lsem,
):
    dp = lax.axis_index("dp")
    tn = lax.axis_index("tensor")
    zl, y = lax.div(dp, 8), lax.rem(dp, 8)
    x, zh, c = lax.div(tn, 8), lax.rem(lax.div(tn, 2), 4), lax.rem(tn, 2)
    zh1, zh0 = lax.div(zh, 2), lax.rem(zh, 2)
    s, q = lax.div(tn, 4), lax.rem(tn, 4)

    def dev(zl_=zl, y_=y, x_=x, zh1_=zh1, zh0_=zh0, c_=c):
        return (zl_ * 8 + y_, x_ * 8 + zh1_ * 4 + zh0_ * 2 + c_)

    def s_dev(s_):
        return dev(x_=lax.div(s_, 2), zh1_=lax.rem(s_, 2))

    flip_zl, flip_c, flip_h = dev(zl_=1 - zl), dev(c_=1 - c), dev(zh0_=1 - zh0)
    flip_zh = dev(zl_=1 - zl, zh0_=1 - zh0)
    flip_h1 = dev(zh1_=1 - zh1)
    line = (flip_h, flip_zl, flip_zh)

    count = [0]
    pending = []

    def sems(n=1):
        first = count[0]
        count[0] += n
        return first

    def rcopy(src, dst, i, target):
        return pltpu.make_async_remote_copy(
            src_ref=src, dst_ref=dst, send_sem=ssem.at[i], recv_sem=rsem.at[i],
            device_id=target, device_id_type=MESH,
        )

    def send(src, dst, i, target):
        copy = rcopy(src, dst, i, target)
        copy.start()
        pending.append(copy)

    def arrived(dst, i):
        rcopy(dst, dst, i, flip_c).wait_recv()

    def column(index):
        return pl.ds(pl.multiple_of(index * 128, 128), 128)

    def stage(src, dst, i):
        copy = pltpu.make_async_copy(src, dst, lsem.at[i])
        copy.start()
        return copy

    hid_in = stage(hid_any, hid, 0)
    key_in = stage(k_any, kvg.at[y, :, pl.ds(0, 128)], 1)
    value_in = stage(v_any, kvg.at[y, :, pl.ds(128, 128)], 2)
    query_in = stage(q_any, qg.at[y], 3)
    out_in = stage(o_any, og.at[:, column(y)], 4)
    own_target = tgt_any.at[:, column((zl * 8 + s) * 4 + q)]
    target_in = stage(own_target, tg.at[zl], 5)

    lo_t = lax.div(tn, 16)
    lo_s = lax.div(lax.rem(tn, 16), 2)
    lo_q = 2 * lax.rem(tn, 2)

    def lo_source(slot):
        return (lo_t * 8 + y, lo_s * 4 + lo_q + slot)

    perm_from = (lax.rem(lax.div(tn, 2) + 8, 16), 2 * dp + c)
    perm_to = (lax.div(tn, 2), 2 * lax.rem(dp + 8, 16) + c)
    greeted = [dev(y_=lax.rem(y + 1, 8)), dev(y_=lax.rem(y + 7, 8))]
    greeted += [flip_zl, flip_c, flip_h, flip_zh]
    greeted += [s_dev(lax.rem(s + d, 8)) for d in range(1, 8)]

    def zh_dev(d):
        other = lax.rem(zh + d, 4)
        return dev(zh1_=lax.div(other, 2), zh0_=lax.rem(other, 2))

    def x_dev(d):
        return dev(x_=lax.rem(x + d, 4))

    greeted += [zh_dev(d) for d in range(1, 4)]
    greeted += [perm_from, lo_source(0), lo_source(1)]
    barrier = pltpu.get_barrier_semaphore()
    for target in greeted:
        pl.semaphore_signal(barrier, inc=1, device_id=target, device_id_type=MESH)

    key_in.wait()
    value_in.wait()
    query_in.wait()
    pl.semaphore_wait(barrier, len(greeted))

    class Ring:
        def __init__(self, part, chunks):
            self.part, self.chunks = part, chunks
            self.base = sems(8 * chunks)

        def live(self, k, d, ch):
            if k < 3:
                return True
            return d == 0 if self.chunks == 1 else d == ch

        def block(self, k, d):
            return lax.rem(y + (8 - k if d == 0 else k), 8)

        def sem(self, k, d, ch):
            return self.base + (k * 2 + d) * self.chunks + ch

        def send(self, k, d, ch):
            ref = self.part(self.block(k, d), ch)
            to = dev(y_=lax.rem(y + (1 if d == 0 else 7), 8))
            send(ref, ref, self.sem(k, d, ch), to)

        def start(self, chunks=None):
            for ch in range(self.chunks) if chunks is None else chunks:
                for d in range(2):
                    self.send(0, d, ch)

        def step(self, k, chunks=None):
            for ch in range(self.chunks) if chunks is None else chunks:
                for d in range(2):
                    if self.live(k, d, ch):
                        arrived(self.part(self.block(k + 1, d), ch), self.sem(k, d, ch))
                        if k < 3 and self.live(k + 1, d, ch):
                            self.send(k + 1, d, ch)

    kv_ring = Ring(lambda b, ch: kvg.at[b, pl.ds(ch * 64, 64)], 2)
    q_ring = Ring(lambda b, ch: qg.at[b, pl.ds(ch * 64, 64)], 2)
    o_ring = Ring(lambda b, ch: og.at[pl.ds(ch * 512, 512), column(b)], 2)
    dt_ring = Ring(lambda b, ch: dtb.at[b, pl.ds(ch * 8, 8)], 2)
    dx_ring = Ring(lambda b, ch: dxb.at[b, ch], 2)
    loss_ring = Ring(lambda b, ch: lring.at[b], 1)

    h_sem, t_sem, dt_sem, p_sem = sems(), sems(), sems(), sems()
    kv_ring.start()
    q_ring.start()
    steps = dtw_ref[...].astype(F32)
    for r in range(8):
        lanes = slice((r % 4) * 128, (r % 4 + 1) * 128)
        dtb[y, pl.ds(zl * 8 + r, 1), :] = steps[r // 4:r // 4 + 1, lanes]
    dt_own = dtb.at[y, pl.ds(pl.multiple_of(zl * 8, 8), 8)]
    send(dt_own, dt_own, dt_sem, flip_zl)
    hid_in.wait()
    for i in range(NY):
        hs[:, pl.ds(i * 128, 128)] = hid[:, column(((1 - zl) * 8 + i) * 4 + q)]
    send(hs, hx.at[zl], h_sem, flip_zl)
    kv_ring.step(0)
    tile = hid[:, pl.ds(pl.multiple_of(tn * 256, 256), 256)]
    ht[...] = tile.astype(F32).T.astype(BF16)
    send(ht, hg.at[c, lax.rem(dp + 8, 16)], p_sem, perm_to)
    for i in range(NY):
        hx[zl, :, pl.ds(i * 128, 128)] = hid[:, column((zl * 8 + i) * 4 + q)]
    q_ring.step(0, [0])
    kv_ring.step(1)
    q_ring.step(0, [1])

    def rows_of(i):
        lanes = column(i)
        return jnp.concatenate([hx[0, :, lanes], hx[1, :, lanes]], axis=0)

    def q_pair(k):
        up, down = lax.rem(y + k, 8), lax.rem(y + 8 - k, 8)
        rows_up, rows_down = rows_of(up), rows_of(down)
        for j in range(4):
            lanes = pl.ds(j * 256, 256)
            cacc[j] += dot(rows_up, qg[up, :, lanes]) + dot(rows_down, qg[down, :, lanes])

    arrived(hx.at[1 - zl], h_sem)
    arrived(dtb.at[y, pl.ds(pl.multiple_of((1 - zl) * 8, 8), 8)], dt_sem)
    dt_ring.start()
    other_target = tgt_any.at[:, column(((1 - zl) * 8 + s) * 4 + q)]
    send(other_target, tg.at[zl], t_sem, flip_zl)
    rows = rows_of(y)
    for j in range(4):
        cacc[j] = dot(rows, qg[y, :, pl.ds(j * 256, 256)])
    q_ring.step(1, [0])
    kv_ring.step(2)
    q_ring.step(1, [1])
    q_pair(1)
    dt_ring.step(0)
    out_in.wait()
    q_ring.step(2, [0])
    kv_ring.step(3)
    q_ring.step(2, [1])
    o_ring.start()
    k1_sem, k2_sem, k3_sem, k4_sem = sems(), sems(3), sems(7), sems()
    rows = jnp.concatenate([hx[0], hx[1]], axis=0)
    kvacc[...] = dot(rows, kvg[...].reshape(1024, 256))
    for zz in range(2):
        kvp[zz] = kvacc[pl.ds(pl.multiple_of(zz * 128 + (1 - c) * 64, 64), 64), :].astype(BF16)
    send(kvp, kvr1, k1_sem, flip_c)
    dt_ring.step(1)
    arrived(kvr1, k1_sem)
    for zz in range(2):
        part = kvacc[pl.ds(pl.multiple_of(zz * 128 + c * 64, 64), 64), :] + kvr1[zz].astype(F32)
        kvt[zz] = part
        kvs[zz] = part.astype(BF16)
    send(kvs.at[1 - zl], kvr2.at[2], k2_sem + 2, flip_zh)
    send(kvs.at[zl], kvr2.at[0], k2_sem, flip_h)
    send(kvs.at[1 - zl], kvr2.at[1], k2_sem + 1, flip_zl)
    q_pair(2)
    dt_ring.step(2)
    q_ring.step(3)
    for j in range(3):
        arrived(kvr2.at[j], k2_sem + j)
    kvall[c, s] = (
        kvt[zl] + kvr2[0].astype(F32) + kvr2[1].astype(F32) + kvr2[2].astype(F32)
    ).astype(BF16)
    own_kv = kvall.at[c, s]
    for d in (1, 3, 5, 7, 2, 4, 6):
        send(own_kv, own_kv, k3_sem + d - 1, s_dev(lax.rem(s + d, 8)))

    class Sum8:
        def __init__(self, acc, p1, r1, p2, r2):
            self.acc, self.p1, self.r1, self.p2, self.r2 = acc, p1, r1, p2, r2
            self.s1, self.s2 = sems(), sems(3)

        def first(self, add):
            for hh in range(2):
                part = self.acc[hh * 2 + 1 - c] + add(hh * 2 + 1 - c)
                for zz in range(2):
                    self.p1[zz, hh] = part[zz * 128:(zz + 1) * 128].astype(BF16)
            send(self.p1, self.r1, self.s1, flip_c)
            for hh in range(2):
                self.acc[hh * 2 + c] += add(hh * 2 + c)

        def second(self):
            arrived(self.r1, self.s1)
            for zz in range(2):
                for hh in range(2):
                    rows = pl.ds(zz * 128, 128)
                    part = self.acc[hh * 2 + c, rows, :] + self.r1[zz, hh].astype(F32)
                    self.acc[hh * 2 + c, rows, :] = part
                    self.p2[zz, hh] = part.astype(BF16)
            send(self.p2.at[1 - zl, 1 - zh0], self.r2.at[2], self.s2 + 2, flip_zh)
            send(self.p2.at[zl, 1 - zh0], self.r2.at[0], self.s2, flip_h)
            send(self.p2.at[1 - zl, zh0], self.r2.at[1], self.s2 + 1, flip_zl)

        def third(self):
            for j in range(3):
                arrived(self.r2.at[j], self.s2 + j)
            own = self.acc[zh0 * 2 + c, pl.ds(pl.multiple_of(zl * 128, 128), 128), :]
            return own + self.r2[0].astype(F32) + self.r2[1].astype(F32) + self.r2[2].astype(F32)

    c_sum = Sum8(cacc, cp1, cr1, cp2, cr2)
    d_sum = Sum8(dacc, dp1, dr1, dp2, dr2)

    last = [lax.rem(y + k, 8) for k in (3, 4, 5)]
    last_rows = [rows_of(i) for i in last]

    def last_q(k):
        lanes = pl.ds(pl.multiple_of(k * 256, 256), 256)
        return sum(dot(r, qg[i, :, lanes]) for r, i in zip(last_rows, last))

    c_sum.first(last_q)
    o_ring.step(0, [0])
    c_sum.second()
    dt_ring.step(3)
    o_ring.step(0, [1])
    w2[...] = jnp.zeros_like(w2)
    for m in range(16):
        for j in range(4):
            for h in range(2):
                w2[h:h + 1, pl.ds((m * 4 + j) * 128, 128)] = dtb[
                    m % 8, pl.ds((m // 8) * 8 + h * 4 + j, 1), :
                ]

    hz_sem = sems(3)
    own_tile = hg.at[c, lax.div(tn, 2)]
    arrived(own_tile, p_sem)
    for d in range(1, 4):
        send(own_tile, own_tile, hz_sem + d - 1, zh_dev(d))
    o_ring.step(1, [0])
    best = dict(precision=lax.Precision.HIGHEST)
    weights = w2[...].astype(BF16)

    def softplus(v):
        return jnp.maximum(v, 0.0) + jnp.log1p(jnp.exp(-jnp.abs(v)))

    step_col = softplus(dot_t(hid[...], weights))
    step_row = softplus(dot_t(weights, hid[...]))
    dtc[...] = step_col
    rate0, rate1 = rate_ref[0], rate_ref[1]
    n_lane = step_col.shape[1]
    lane = lax.broadcasted_iota(jnp.int32, (TOK, n_lane), 1)
    subl = lax.broadcasted_iota(jnp.int32, (n_lane, TOK), 0)
    at_t = lax.broadcasted_iota(jnp.int32, (TOK, TOK), 0)
    at_j = lax.broadcasted_iota(jnp.int32, (TOK, TOK), 1)
    lower = (at_j <= at_t).astype(F32)
    upper = (at_t <= at_j).astype(F32)
    cs_col = dot(lower, step_col * jnp.where(lane == 0, rate0, rate1), **best)
    cs_row = dot(step_row * jnp.where(subl == 0, rate0, rate1), upper, **best)
    seg_row = jnp.broadcast_to(seg_ref[...].astype(F32), (TOK, TOK))
    visible = (seg_row == seg_row.T) & (at_j <= at_t)
    for h in range(2):
        distance = jnp.where(visible, cs_col[:, h:h + 1] - cs_row[h:h + 1, :], 0.0)
        mix[h] = jnp.where(visible, jnp.exp(-distance), 0.0)

    o_ring.step(1, [1])
    for d in range(1, 8):
        arrived(kvall.at[c, lax.rem(s + 8 - d, 8)], k3_sem + d - 1)
    send(kvall.at[c], kvall.at[c], k4_sem, flip_c)
    y_sem, y2_sem = sems(3), sems()
    c_full = (c_sum.third() * (128 ** -0.5)).astype(BF16)
    arrived(kvall.at[1 - c], k4_sem)
    for h in range(2):
        head = map_ref[h]
        both = jnp.concatenate([kvall[0, head], kvall[1, head]], axis=0)
        scores = dot_t(c_full[:, h * 128:(h + 1) * 128], both[:, :128])
        mixing = scores * mix[h]
        mix[h] = mixing
        source = dtc[:, h:h + 1] * both[:, 128:].astype(F32)
        yb[c, zl, zh0, :, pl.ds(h * 128, 128)] = dot(mixing, source, **best).astype(BF16)
    hx_sem = sems(3)
    own_y = yb.at[c, zl, zh0]
    send(own_y, own_y, y_sem + 2, flip_zh)
    send(own_y, own_y, y_sem, flip_h)
    send(own_y, own_y, y_sem + 1, flip_zl)
    o_ring.step(2)
    arrived(yb.at[c, zl, 1 - zh0], y_sem)
    arrived(yb.at[c, 1 - zl, zh0], y_sem + 1)
    arrived(yb.at[c, 1 - zl, 1 - zh0], y_sem + 2)
    send(yb.at[c], yb.at[c], y2_sem, flip_c)
    hc_sem = sems()
    for d in range(1, 4):
        arrived(hg.at[c, x * 4 + lax.rem(zh + 4 - d, 4)], hz_sem + d - 1)
    o_ring.step(3)
    arrived(yb.at[1 - c], y2_sem)
    for zz in range(2):
        for hh in range(2):
            for cc in range(2):
                ycat[pl.ds(zz * 128, 128), pl.ds((hh * 2 + cc) * 256, 256)] = yb[cc, zz, hh]

    l0_sem, l1_sem, l2_sem = sems(3), sems(3), sems()
    for d in (2, 1, 3, 0):
        at = lax.rem(x + d, 4)
        value = dot(ycat[...], og[:, pl.ds(pl.multiple_of(at * 256, 256), 256)])
        if d:
            lp[at, 0] = value[:, :128].astype(BF16)
            lp[at, 1] = value[:, 128:].astype(BF16)
            send(lp.at[at, 1 - zh1], lr1.at[1, d - 1], l0_sem + d - 1, x_dev(d))
        else:
            lt[0] = value[:, :128]
            lt[1] = value[:, 128:]
    for d in (2, 1, 3):
        at = lax.rem(x + d, 4)
        send(lp.at[at, zh1], lr1.at[0, d - 1], l1_sem + d - 1, x_dev(d))
    for d in range(3):
        arrived(lr1.at[1, d], l0_sem + d)
    ls[...] = (
        lt[1 - zh1] + lr1[1, 0].astype(F32) + lr1[1, 1].astype(F32) + lr1[1, 2].astype(F32)
    ).astype(BF16)
    send(ls, lr2, l2_sem, flip_h1)
    for d in range(3):
        arrived(lr1.at[0, d], l1_sem + d)
    near = lt[zh1] + lr1[0, 0].astype(F32) + lr1[0, 1].astype(F32) + lr1[0, 2].astype(F32)
    target_in.wait()
    arrived(tg.at[1 - zl], t_sem)
    arrived(lr2, l2_sem)
    layer = (near + lr2[...].astype(F32)).astype(BF16)
    g1_sem, g2_sem, g3_sem, la_sem, la2_sem = sems(), sems(3), sems(3), sems(), sems(3)
    squares = jnp.zeros((8, 128), F32)
    for zz in range(2):
        rows = layer[zz * 128:(zz + 1) * 128]
        lob[zz] = rows
        residual = rows.astype(F32) - tg[zz].astype(F32)
        gob[pl.ds(zz * 128, 128), column(s)] = (2.0 * residual / TOKENS).astype(BF16)
        squares += jnp.sum((residual * residual).reshape(16, 8, 128), axis=0)
    lsa[s] = squares
    own_g = gob.at[:, column(s)]
    send(own_g, own_g, g1_sem, flip_h1)
    for d in (2, 1, 3):
        send(own_g, own_g, g2_sem + d - 1, x_dev(d))
    send(lsa.at[s], lsa.at[s], la_sem, flip_h1)
    next_g = gob.at[:, column(2 * x + 1 - zh1)]
    arrived(next_g, g1_sem)
    for d in (2, 1, 3):
        send(next_g, next_g, g3_sem + d - 1, x_dev(d))
    arrived(lsa.at[2 * x + 1 - zh1], la_sem)
    loss_pair = lsa.at[pl.ds(x * 2, 2)]
    for d in range(1, 4):
        send(loss_pair, loss_pair, la2_sem + d - 1, x_dev(d))

    lo_sem = sems(2)
    lo_tn = 16 * zl + 2 * s + lax.div(q, 2)
    slot = lax.rem(q, 2)
    lo_dst = lo_ref.at[:, column(slot)]
    lo_copies = []
    for zz in range(2):
        to = (zz * 8 + y, lo_tn)
        here = (zl == zz) & (lo_tn == tn)
        copy = pltpu.make_async_remote_copy(
            src_ref=lob.at[zz], dst_ref=lo_dst, send_sem=ssem.at[lo_sem + zz],
            recv_sem=rsem.at[lo_sem + slot], device_id=to, device_id_type=MESH,
        )
        lo_copies.append((copy, here))

        @pl.when(here)
        def _():
            lo_ref[:, column(slot)] = lob[zz]

        @pl.when(jnp.logical_not(here))
        def _():
            copy.start()

    def d_part(at):
        lanes = pl.ds(pl.multiple_of(at * 256, 256), 256)
        rows = gob[:, lanes]

        def part(k):
            return dot_t(rows, og[pl.ds(pl.multiple_of(k * 256, 256), 256), lanes])
        return part

    quad = hg.at[c, pl.ds(x * 4, 4)]
    for d in range(1, 4):
        send(quad, quad, hx_sem + d - 1, x_dev(d))
    part = d_part(x)
    for k in range(4):
        dacc[k] = part(k)
    for d in (1, 3, 2):
        at = lax.rem(x + 4 - d, 4)
        arrived(gob.at[:, column(at * 2 + zh1)], g2_sem + d - 1)
        arrived(gob.at[:, column(at * 2 + 1 - zh1)], g3_sem + d - 1)
        part = d_part(at)
        if d == 2:
            d_sum.first(part)
        else:
            for k in range(4):
                dacc[k] += part(k)
    lb_sem, lc_sem = sems(), sems(3)
    for d in range(1, 4):
        arrived(lsa.at[pl.ds(lax.rem(x + 4 - d, 4) * 2, 2)], la2_sem + d - 1)
    total = lsa[0]
    for i in range(1, 8):
        total += lsa[i]
    lsb[...] = total
    send(lsb, lsb1, lb_sem, flip_c)
    d_sum.second()
    arrived(lsb1, lb_sem)
    lsc[...] = lsb[...] + lsb1[...]
    for j in range(3):
        send(lsc, lsc2.at[j], lc_sem + j, line[j])
    for d in range(1, 4):
        arrived(hg.at[c, pl.ds(lax.rem(x + 4 - d, 4) * 4, 4)], hx_sem + d - 1)
    send(hg.at[c], hg.at[c], hc_sem, flip_c)
    dy = d_sum.third().astype(BF16).astype(F32)
    dx_sem = sems()
    for h in range(2):
        back = dot(mix[h].T, dy[:, h * 128:(h + 1) * 128], **best)
        dxb[y, zl, :, pl.ds(h * 128, 128)] = (dtc[:, h:h + 1] * back).astype(BF16)
    send(dxb.at[y, zl], dxb.at[y, zl], dx_sem, flip_zl)
    dx_ring.start([zl])
    for j in range(3):
        arrived(lsc2.at[j], lc_sem + j)
    lring[y] = lsc[...] + lsc2[0] + lsc2[1] + lsc2[2]
    arrived(dxb.at[y, 1 - zl], dx_sem)
    dx_ring.start([1 - zl])
    loss_ring.start()
    arrived(hg.at[1 - c], hc_sem)

    def g_block(i, first=False):
        grads = jnp.concatenate([dxb[i, 0], dxb[i, 1]], axis=0)
        for b in range(2):
            tokens = jnp.concatenate([hg[b, 8 + i], hg[b, i]], axis=1)
            rows = pl.ds(b * 256, 256)
            if first:
                gx_ref[rows, :] = dot(tokens, grads)
            else:
                gx_ref[rows, :] += dot(tokens, grads)

    g_block(y, True)
    for k in range(4):
        dx_ring.step(k)
        loss_ring.step(k)
        g_block(lax.rem(y + 7 - k, 8))
        if k < 3:
            g_block(lax.rem(y + k + 1, 8))
    total = jnp.sum(jnp.sum(lring[...], axis=0), axis=0, keepdims=True)
    total = jnp.sum(total, axis=1, keepdims=True) / (TOKENS * WIDTH)
    loss_ref[...] = total

    for copy in pending:
        copy.wait_send()
    for copy, here in lo_copies:
        @pl.when(jnp.logical_not(here))
        def _():
            copy.wait_send()
    for k in range(2):
        from_dp, from_tn = lo_source(k)
        here = (from_dp == dp) & (from_tn == tn)

        @pl.when(jnp.logical_not(here))
        def _():
            arrived(lo_ref.at[:, pl.ds(k * 128, 128)], lo_sem + k)


def store(lo_in, gx_in, loss_in, lo_out, gx_out, loss_out, sem):
    moves = [
        pltpu.make_async_copy(src, dst, sem.at[i])
        for i, (src, dst) in enumerate(((gx_in, gx_out), (lo_in, lo_out), (loss_in, loss_out)))
    ]
    for move in moves:
        move.start()
    for move in moves:
        move.wait()


def local(
    hidden, target, segments, head_map, decay_rate, dt_weight,
    teacher_query, teacher_key, teacher_value, teacher_out,
):
    steps = dt_weight.T
    anywhere = pl.BlockSpec(memory_space=pltpu.HBM)
    vmem = pl.BlockSpec(memory_space=pltpu.VMEM)
    smem = pl.BlockSpec(memory_space=pltpu.SMEM)

    def b(*shape):
        return pltpu.VMEM(shape, BF16)

    def f(*shape):
        return pltpu.VMEM(shape, F32)

    scratch = [
        b(128, 8192), b(2, 128, 128), b(8, 128, 1024), b(8, 128, 256), b(1024, 1024),
        f(8, 16, 128), b(2, 128, 1024), b(128, 1024), b(256, 128), b(2, 16, 256, 128),
        f(256, 256), b(2, 64, 256), b(2, 64, 256), f(2, 64, 256), b(2, 64, 256), b(3, 64, 256),
        b(2, 8, 64, 256),
        f(4, 256, 256), b(2, 2, 128, 256), b(2, 2, 128, 256), b(2, 2, 128, 256), b(3, 128, 256),
        f(16, 8192), f(2, 128, 128), f(128, 16), b(2, 2, 2, 128, 256), b(256, 1024),
        b(4, 2, 256, 128), b(2, 3, 256, 128), f(2, 256, 128), b(256, 128),
        b(256, 128), b(2, 128, 128),
        b(256, 1024), f(4, 256, 256), b(2, 2, 128, 256), b(2, 2, 128, 256),
        b(2, 2, 128, 256), b(3, 128, 256), b(8, 2, 128, 256),
        f(8, 8, 128), f(8, 128), f(8, 128), f(8, 128), f(3, 8, 128), f(8, 8, 128),
        pltpu.SemaphoreType.DMA((N_SEM,)), pltpu.SemaphoreType.DMA((N_SEM,)),
        pltpu.SemaphoreType.DMA((6,)),
    ]
    layer_out, grad_x, loss = pl.pallas_call(
        kernel,
        out_shape=(
            jax.ShapeDtypeStruct((128, 256), BF16),
            jax.ShapeDtypeStruct((512, 256), F32),
            jax.ShapeDtypeStruct((1, 1), F32),
        ),
        in_specs=[anywhere, anywhere, vmem, smem, smem, vmem] + [anywhere] * 4,
        out_specs=(vmem, vmem, vmem),
        scratch_shapes=scratch,
        compiler_params=pltpu.CompilerParams(
            collective_id=0, has_side_effects=True, vmem_limit_bytes=65536 * 1024 - 640 * 1024
        ),
    )(
        hidden, target, segments, head_map, decay_rate, steps,
        teacher_query[0], teacher_key[0], teacher_value[0], teacher_out[0],
    )
    layer_out, grad_x, loss = pl.pallas_call(
        store,
        out_shape=(
            jax.ShapeDtypeStruct((128, 256), BF16),
            jax.ShapeDtypeStruct((512, 256), F32),
            jax.ShapeDtypeStruct((1, 1), F32),
        ),
        in_specs=[anywhere] * 3,
        out_specs=(anywhere,) * 3,
        scratch_shapes=[pltpu.SemaphoreType.DMA((3,))],
    )(layer_out, grad_x, loss)
    return layer_out, grad_x, loss[0, 0]


def solution(mesh):
    in_specs = (
        P("dp", None),
        P("dp", None),
        P("dp", None),
        P("tensor"),
        P("tensor"),
        P("dp", "tensor"),
        P("tensor", "dp", None),
        P("tensor", "dp", None),
        P("tensor", "dp", None),
        P("tensor", None, "dp"),
    )
    out_specs = (P("dp", "tensor"), P("dp", "tensor"), P())
    return jax.shard_map(local, mesh=mesh, in_specs=in_specs, out_specs=out_specs, check_vma=False)
```

```python
import jax
import jax.numpy as jnp
from jax import lax
from jax.experimental import pallas as pl
from jax.experimental.pallas import tpu as pltpu
from jax.sharding import PartitionSpec as P

F32 = jnp.float32
BF16 = jnp.bfloat16
MESH = pl.DeviceIdType.MESH
TOK = 128
TOKENS = 2048
WIDTH = 8192
NY = 8
N_SEM = 192


def dot(a, b, **kw):
    return jnp.dot(a, b, preferred_element_type=F32, **kw)


def dot_t(a, b, **kw):
    return lax.dot_general(a, b, (((1,), (1,)), ((), ())), preferred_element_type=F32, **kw)


def kernel(
    hid_any, tgt_any, seg_ref, map_ref, rate_ref, dtw_ref, q_any, k_any, v_any, o_any,
    lo_ref, gx_ref, loss_ref,
    hid, tg, qg, kvg, og, dtb, hx, hs, ht, hg,
    kvacc, kvp, kvr1, kvt, kvs, kvr2, kvall,
    cacc, cp1, cr1, cp2, cr2,
    w2, mix, dtc, yb, ycat,
    lp, lr1, lt, ls, lr2, lob,
    gob, dacc, dp1, dr1, dp2, dr2, dxb,
    lsa, lsb, lsb1, lsc, lsc2, lring,
    ssem, rsem, lsem,
):
    dp = lax.axis_index("dp")
    tn = lax.axis_index("tensor")
    zl, y = lax.div(dp, 8), lax.rem(dp, 8)
    x, zh, c = lax.div(tn, 8), lax.rem(lax.div(tn, 2), 4), lax.rem(tn, 2)
    zh1, zh0 = lax.div(zh, 2), lax.rem(zh, 2)
    s, q = lax.div(tn, 4), lax.rem(tn, 4)

    def dev(zl_=zl, y_=y, x_=x, zh1_=zh1, zh0_=zh0, c_=c):
        return (zl_ * 8 + y_, x_ * 8 + zh1_ * 4 + zh0_ * 2 + c_)

    def s_dev(s_):
        return dev(x_=lax.div(s_, 2), zh1_=lax.rem(s_, 2))

    flip_zl, flip_c, flip_h = dev(zl_=1 - zl), dev(c_=1 - c), dev(zh0_=1 - zh0)
    flip_zh = dev(zl_=1 - zl, zh0_=1 - zh0)
    flip_h1 = dev(zh1_=1 - zh1)
    line = (flip_h, flip_zl, flip_zh)

    count = [0]
    pending = []

    def sems(n=1):
        first = count[0]
        count[0] += n
        return first

    def rcopy(src, dst, i, target):
        return pltpu.make_async_remote_copy(
            src_ref=src, dst_ref=dst, send_sem=ssem.at[i], recv_sem=rsem.at[i],
            device_id=target, device_id_type=MESH,
        )

    def send(src, dst, i, target):
        copy = rcopy(src, dst, i, target)
        copy.start()
        pending.append(copy)

    def arrived(dst, i):
        rcopy(dst, dst, i, flip_c).wait_recv()

    def column(index):
        return pl.ds(pl.multiple_of(index * 128, 128), 128)

    def stage(src, dst, i):
        copy = pltpu.make_async_copy(src, dst, lsem.at[i])
        copy.start()
        return copy

    lo_t = lax.div(tn, 16)
    lo_s = lax.div(lax.rem(tn, 16), 2)
    lo_q = 2 * lax.rem(tn, 2)

    def lo_source(slot):
        return (lo_t * 8 + y, lo_s * 4 + lo_q + slot)

    perm_from = (lax.rem(lax.div(tn, 2) + 8, 16), 2 * dp + c)
    perm_to = (lax.div(tn, 2), 2 * lax.rem(dp + 8, 16) + c)
    greeted = [dev(y_=lax.rem(y + 1, 8)), dev(y_=lax.rem(y + 7, 8))]
    greeted += [flip_zl, flip_c, flip_h, flip_zh]
    greeted += [s_dev(lax.rem(s + d, 8)) for d in range(1, 8)]

    def zh_dev(d):
        other = lax.rem(zh + d, 4)
        return dev(zh1_=lax.div(other, 2), zh0_=lax.rem(other, 2))

    def x_dev(d):
        return dev(x_=lax.rem(x + d, 4))

    greeted += [zh_dev(d) for d in range(1, 4)]
    greeted += [perm_from, lo_source(0), lo_source(1)]
    barrier = pltpu.get_barrier_semaphore()
    for target in greeted:
        pl.semaphore_signal(barrier, inc=1, device_id=target, device_id_type=MESH)

    hid_in = stage(hid_any, hid, 0)
    key_in = stage(k_any, kvg.at[y, :, pl.ds(0, 128)], 1)
    value_in = stage(v_any, kvg.at[y, :, pl.ds(128, 128)], 2)
    query_in = stage(q_any, qg.at[y], 3)
    out_in = stage(o_any, og.at[:, column(y)], 4)
    own_target = tgt_any.at[:, column((zl * 8 + s) * 4 + q)]
    target_in = stage(own_target, tg.at[zl], 5)

    key_in.wait()
    value_in.wait()
    query_in.wait()
    pl.semaphore_wait(barrier, len(greeted))

    class Ring:
        def __init__(self, part, chunks):
            self.part, self.chunks = part, chunks
            self.base = sems(8 * chunks)

        def live(self, k, d, ch):
            if k < 3:
                return True
            return d == 0 if self.chunks == 1 else d == ch

        def block(self, k, d):
            return lax.rem(y + (8 - k if d == 0 else k), 8)

        def sem(self, k, d, ch):
            return self.base + (k * 2 + d) * self.chunks + ch

        def send(self, k, d, ch):
            ref = self.part(self.block(k, d), ch)
            to = dev(y_=lax.rem(y + (1 if d == 0 else 7), 8))
            send(ref, ref, self.sem(k, d, ch), to)

        def start(self, chunks=None):
            for ch in range(self.chunks) if chunks is None else chunks:
                for d in range(2):
                    self.send(0, d, ch)

        def step(self, k, chunks=None):
            for ch in range(self.chunks) if chunks is None else chunks:
                for d in range(2):
                    if self.live(k, d, ch):
                        arrived(self.part(self.block(k + 1, d), ch), self.sem(k, d, ch))
                        if k < 3 and self.live(k + 1, d, ch):
                            self.send(k + 1, d, ch)

    kv_ring = Ring(lambda b, ch: kvg.at[b, pl.ds(ch * 64, 64)], 2)
    q_ring = Ring(lambda b, ch: qg.at[b, pl.ds(ch * 64, 64)], 2)
    o_ring = Ring(lambda b, ch: og.at[pl.ds(ch * 512, 512), column(b)], 2)
    dt_ring = Ring(lambda b, ch: dtb.at[b, pl.ds(ch * 8, 8)], 2)
    dx_ring = Ring(lambda b, ch: dxb.at[b, 1 - zl if ch else zl], 2)
    loss_ring = Ring(lambda b, ch: lring.at[b], 1)

    h_sem, t_sem, dt_sem, p_sem = sems(), sems(), sems(), sems()
    kv_ring.start()
    q_ring.start()
    steps = dtw_ref[...].astype(F32)
    for r in range(8):
        lanes = slice((r % 4) * 128, (r % 4 + 1) * 128)
        dtb[y, pl.ds(zl * 8 + r, 1), :] = steps[r // 4:r // 4 + 1, lanes]
    dt_own = dtb.at[y, pl.ds(pl.multiple_of(zl * 8, 8), 8)]
    send(dt_own, dt_own, dt_sem, flip_zl)
    hid_in.wait()
    for i in range(NY):
        hs[:, pl.ds(i * 128, 128)] = hid[:, column(((1 - zl) * 8 + i) * 4 + q)]
    send(hs, hx.at[zl], h_sem, flip_zl)
    kv_ring.step(0)
    tile = hid[:, pl.ds(pl.multiple_of(tn * 256, 256), 256)]
    ht[...] = tile.astype(F32).T.astype(BF16)
    send(ht, hg.at[c, lax.rem(dp + 8, 16)], p_sem, perm_to)
    for i in range(NY):
        hx[zl, :, pl.ds(i * 128, 128)] = hid[:, column((zl * 8 + i) * 4 + q)]
    q_ring.step(0, [0])
    kv_ring.step(1)
    q_ring.step(0, [1])

    def rows_of(i):
        lanes = column(i)
        return jnp.concatenate([hx[0, :, lanes], hx[1, :, lanes]], axis=0)

    def q_pair(k):
        up, down = lax.rem(y + k, 8), lax.rem(y + 8 - k, 8)
        rows_up, rows_down = rows_of(up), rows_of(down)
        for j in range(4):
            lanes = pl.ds(j * 256, 256)
            cacc[j] += dot(rows_up, qg[up, :, lanes]) + dot(rows_down, qg[down, :, lanes])

    arrived(hx.at[1 - zl], h_sem)
    arrived(dtb.at[y, pl.ds(pl.multiple_of((1 - zl) * 8, 8), 8)], dt_sem)
    dt_ring.start()
    other_target = tgt_any.at[:, column(((1 - zl) * 8 + s) * 4 + q)]
    send(other_target, tg.at[zl], t_sem, flip_zl)
    rows = rows_of(y)
    for j in range(4):
        cacc[j] = dot(rows, qg[y, :, pl.ds(j * 256, 256)])
    q_ring.step(1, [0])
    kv_ring.step(2)
    q_ring.step(1, [1])
    hz_sem = sems(3)
    own_tile = hg.at[c, lax.div(tn, 2)]
    arrived(own_tile, p_sem)
    for d in range(1, 4):
        send(own_tile, own_tile, hz_sem + d - 1, zh_dev(d))
    q_pair(1)
    dt_ring.step(0)
    out_in.wait()
    q_ring.step(2, [0])
    kv_ring.step(3)
    k1_sem, k2_sem, k3_sem, k4_sem = sems(), sems(3), sems(7), sems()
    rows = jnp.concatenate([hx[0], hx[1]], axis=0)
    kvacc[...] = dot(rows, kvg[...].reshape(1024, 256))
    for zz in range(2):
        kvp[zz] = kvacc[pl.ds(pl.multiple_of(zz * 128 + (1 - c) * 64, 64), 64), :].astype(BF16)
    send(kvp, kvr1, k1_sem, flip_c)
    q_ring.step(2, [1])
    o_ring.start()
    dt_ring.step(1)
    arrived(kvr1, k1_sem)
    for zz in range(2):
        part = kvacc[pl.ds(pl.multiple_of(zz * 128 + c * 64, 64), 64), :] + kvr1[zz].astype(F32)
        kvt[zz] = part
        kvs[zz] = part.astype(BF16)
    send(kvs.at[1 - zl], kvr2.at[2], k2_sem + 2, flip_zh)
    send(kvs.at[zl], kvr2.at[0], k2_sem, flip_h)
    send(kvs.at[1 - zl], kvr2.at[1], k2_sem + 1, flip_zl)
    hx_sem = sems(3)
    for d in range(1, 4):
        arrived(hg.at[c, x * 4 + lax.rem(zh + 4 - d, 4)], hz_sem + d - 1)
    quad = hg.at[c, pl.ds(x * 4, 4)]
    for d in range(1, 4):
        send(quad, quad, hx_sem + d - 1, x_dev(d))
    q_pair(2)
    dt_ring.step(2)
    q_ring.step(3)
    for j in range(3):
        arrived(kvr2.at[j], k2_sem + j)
    kvall[c, s] = (
        kvt[zl] + kvr2[0].astype(F32) + kvr2[1].astype(F32) + kvr2[2].astype(F32)
    ).astype(BF16)
    own_kv = kvall.at[c, s]
    for d in (1, 3, 5, 7, 2, 4, 6):
        send(own_kv, own_kv, k3_sem + d - 1, s_dev(lax.rem(s + d, 8)))

    class Sum8:
        def __init__(self, acc, p1, r1, p2, r2):
            self.acc, self.p1, self.r1, self.p2, self.r2 = acc, p1, r1, p2, r2
            self.s1, self.s2 = sems(), sems(3)

        def first(self, add):
            for hh in range(2):
                part = self.acc[hh * 2 + 1 - c] + add(hh * 2 + 1 - c)
                for zz in range(2):
                    self.p1[zz, hh] = part[zz * 128:(zz + 1) * 128].astype(BF16)
            send(self.p1, self.r1, self.s1, flip_c)
            for hh in range(2):
                self.acc[hh * 2 + c] += add(hh * 2 + c)

        def second(self):
            arrived(self.r1, self.s1)
            for zz in range(2):
                for hh in range(2):
                    rows = pl.ds(zz * 128, 128)
                    part = self.acc[hh * 2 + c, rows, :] + self.r1[zz, hh].astype(F32)
                    self.acc[hh * 2 + c, rows, :] = part
                    self.p2[zz, hh] = part.astype(BF16)
            send(self.p2.at[1 - zl, 1 - zh0], self.r2.at[2], self.s2 + 2, flip_zh)
            send(self.p2.at[zl, 1 - zh0], self.r2.at[0], self.s2, flip_h)
            send(self.p2.at[1 - zl, zh0], self.r2.at[1], self.s2 + 1, flip_zl)

        def third(self):
            for j in range(3):
                arrived(self.r2.at[j], self.s2 + j)
            own = self.acc[zh0 * 2 + c, pl.ds(pl.multiple_of(zl * 128, 128), 128), :]
            return own + self.r2[0].astype(F32) + self.r2[1].astype(F32) + self.r2[2].astype(F32)

    c_sum = Sum8(cacc, cp1, cr1, cp2, cr2)
    d_sum = Sum8(dacc, dp1, dr1, dp2, dr2)

    last = [lax.rem(y + k, 8) for k in (3, 4, 5)]
    last_rows = [rows_of(i) for i in last]

    def last_q(k):
        lanes = pl.ds(pl.multiple_of(k * 256, 256), 256)
        return sum(dot(r, qg[i, :, lanes]) for r, i in zip(last_rows, last))

    c_sum.first(last_q)
    o_ring.step(0, [0])
    c_sum.second()
    dt_ring.step(3)
    o_ring.step(0, [1])
    w2[...] = jnp.zeros_like(w2)
    for m in range(16):
        for j in range(4):
            for h in range(2):
                w2[h:h + 1, pl.ds((m * 4 + j) * 128, 128)] = dtb[
                    m % 8, pl.ds((m // 8) * 8 + h * 4 + j, 1), :
                ]

    o_ring.step(1, [0])
    best = dict(precision=lax.Precision.HIGHEST)
    weights = w2[...].astype(BF16)

    def softplus(v):
        return jnp.maximum(v, 0.0) + jnp.log1p(jnp.exp(-jnp.abs(v)))

    step_col = softplus(dot_t(hid[...], weights))
    step_row = softplus(dot_t(weights, hid[...]))
    dtc[...] = step_col
    rate0, rate1 = rate_ref[0], rate_ref[1]
    n_lane = step_col.shape[1]
    lane = lax.broadcasted_iota(jnp.int32, (TOK, n_lane), 1)
    subl = lax.broadcasted_iota(jnp.int32, (n_lane, TOK), 0)
    at_t = lax.broadcasted_iota(jnp.int32, (TOK, TOK), 0)
    at_j = lax.broadcasted_iota(jnp.int32, (TOK, TOK), 1)
    lower = (at_j <= at_t).astype(F32)
    upper = (at_t <= at_j).astype(F32)
    cs_col = dot(lower, step_col * jnp.where(lane == 0, rate0, rate1), **best)
    cs_row = dot(step_row * jnp.where(subl == 0, rate0, rate1), upper, **best)
    seg_row = jnp.broadcast_to(seg_ref[...].astype(F32), (TOK, TOK))
    visible = (seg_row == seg_row.T) & (at_j <= at_t)
    for h in range(2):
        distance = jnp.where(visible, cs_col[:, h:h + 1] - cs_row[h:h + 1, :], 0.0)
        mix[h] = jnp.where(visible, jnp.exp(-distance), 0.0)

    o_ring.step(1, [1])
    for d in range(1, 8):
        arrived(kvall.at[c, lax.rem(s + 8 - d, 8)], k3_sem + d - 1)
    send(kvall.at[c], kvall.at[c], k4_sem, flip_c)
    y_sem, y2_sem = sems(3), sems()
    c_full = (c_sum.third() * (128 ** -0.5)).astype(BF16)
    arrived(kvall.at[1 - c], k4_sem)
    mixings = []
    for h in range(2):
        head = map_ref[h]
        both = jnp.concatenate([kvall[0, head], kvall[1, head]], axis=0)
        scores = dot_t(c_full[:, h * 128:(h + 1) * 128], both[:, :128])
        mixing = scores * mix[h]
        mixings.append(mixing)
        source = dtc[:, h:h + 1] * both[:, 128:].astype(F32)
        yb[c, zl, zh0, :, pl.ds(h * 128, 128)] = dot(mixing, source, **best).astype(BF16)
    own_y = yb.at[c, zl, zh0]
    send(own_y, own_y, y_sem + 2, flip_zh)
    send(own_y, own_y, y_sem, flip_h)
    send(own_y, own_y, y_sem + 1, flip_zl)
    for h in range(2):
        mix[h] = mixings[h].T
    o_ring.step(2)
    arrived(yb.at[c, zl, 1 - zh0], y_sem)
    arrived(yb.at[c, 1 - zl, zh0], y_sem + 1)
    arrived(yb.at[c, 1 - zl, 1 - zh0], y_sem + 2)
    send(yb.at[c], yb.at[c], y2_sem, flip_c)
    hc_sem = sems()
    o_ring.step(3)
    arrived(yb.at[1 - c], y2_sem)
    for d in range(1, 4):
        arrived(hg.at[c, pl.ds(lax.rem(x + 4 - d, 4) * 4, 4)], hx_sem + d - 1)
    send(hg.at[c], hg.at[c], hc_sem, flip_c)
    for zz in range(2):
        for hh in range(2):
            for cc in range(2):
                ycat[pl.ds(zz * 128, 128), pl.ds((hh * 2 + cc) * 256, 256)] = yb[cc, zz, hh]

    l0_sem, l1_sem, l2_sem = sems(3), sems(3), sems()
    for d in (2, 1, 3, 0):
        at = lax.rem(x + d, 4)
        value = dot(ycat[...], og[:, pl.ds(pl.multiple_of(at * 256, 256), 256)])
        if d:
            lp[at, 0] = value[:, :128].astype(BF16)
            lp[at, 1] = value[:, 128:].astype(BF16)
            send(lp.at[at, 1 - zh1], lr1.at[1, d - 1], l0_sem + d - 1, x_dev(d))
        else:
            lt[0] = value[:, :128]
            lt[1] = value[:, 128:]
    for d in (2, 1, 3):
        at = lax.rem(x + d, 4)
        send(lp.at[at, zh1], lr1.at[0, d - 1], l1_sem + d - 1, x_dev(d))
    for d in range(3):
        arrived(lr1.at[1, d], l0_sem + d)
    ls[...] = (
        lt[1 - zh1] + lr1[1, 0].astype(F32) + lr1[1, 1].astype(F32) + lr1[1, 2].astype(F32)
    ).astype(BF16)
    send(ls, lr2, l2_sem, flip_h1)
    for d in range(3):
        arrived(lr1.at[0, d], l1_sem + d)
    near = lt[zh1] + lr1[0, 0].astype(F32) + lr1[0, 1].astype(F32) + lr1[0, 2].astype(F32)
    target_in.wait()
    arrived(tg.at[1 - zl], t_sem)
    arrived(lr2, l2_sem)
    layer = (near + lr2[...].astype(F32)).astype(BF16)
    g1_sem, g2_sem, g3_sem, la_sem, la2_sem = sems(), sems(3), sems(3), sems(), sems(3)
    squares = jnp.zeros((8, 128), F32)
    for zz in range(2):
        rows = layer[zz * 128:(zz + 1) * 128]
        lob[zz] = rows
        residual = rows.astype(F32) - tg[zz].astype(F32)
        gob[pl.ds(zz * 128, 128), column(s)] = (2.0 * residual / TOKENS).astype(BF16)
        squares += jnp.sum((residual * residual).reshape(16, 8, 128), axis=0)
    lsa[s] = squares
    own_g = gob.at[:, column(s)]
    send(own_g, own_g, g1_sem, flip_h1)
    for d in (2, 1, 3):
        send(own_g, own_g, g2_sem + d - 1, x_dev(d))
    send(lsa.at[s], lsa.at[s], la_sem, flip_h1)
    next_g = gob.at[:, column(2 * x + 1 - zh1)]
    arrived(next_g, g1_sem)
    for d in (2, 1, 3):
        send(next_g, next_g, g3_sem + d - 1, x_dev(d))
    arrived(lsa.at[2 * x + 1 - zh1], la_sem)
    loss_pair = lsa.at[pl.ds(x * 2, 2)]
    for d in range(1, 4):
        send(loss_pair, loss_pair, la2_sem + d - 1, x_dev(d))

    lo_sem = sems(2)
    lo_tn = 16 * zl + 2 * s + lax.div(q, 2)
    slot = lax.rem(q, 2)
    lo_dst = lo_ref.at[:, column(slot)]
    lo_copies = []
    for zz in range(2):
        to = (zz * 8 + y, lo_tn)
        here = (zl == zz) & (lo_tn == tn)
        copy = pltpu.make_async_remote_copy(
            src_ref=lob.at[zz], dst_ref=lo_dst, send_sem=ssem.at[lo_sem + zz],
            recv_sem=rsem.at[lo_sem + slot], device_id=to, device_id_type=MESH,
        )
        lo_copies.append((copy, here))

        @pl.when(here)
        def _():
            lo_ref[:, column(slot)] = lob[zz]

        @pl.when(jnp.logical_not(here))
        def _():
            copy.start()

    def d_part(at):
        lanes = pl.ds(pl.multiple_of(at * 256, 256), 256)
        rows = gob[:, lanes]

        def part(k):
            return dot_t(rows, og[pl.ds(pl.multiple_of(k * 256, 256), 256), lanes])
        return part

    part = d_part(x)
    for k in range(4):
        dacc[k] = part(k)
    for d in (1, 3, 2):
        at = lax.rem(x + 4 - d, 4)
        arrived(gob.at[:, column(at * 2 + zh1)], g2_sem + d - 1)
        arrived(gob.at[:, column(at * 2 + 1 - zh1)], g3_sem + d - 1)
        part = d_part(at)
        if d == 2:
            d_sum.first(part)
        else:
            for k in range(4):
                dacc[k] += part(k)
    lb_sem, lc_sem = sems(), sems(3)
    for d in range(1, 4):
        arrived(lsa.at[pl.ds(lax.rem(x + 4 - d, 4) * 2, 2)], la2_sem + d - 1)
    total = lsa[0]
    for i in range(1, 8):
        total += lsa[i]
    lsb[...] = total
    send(lsb, lsb1, lb_sem, flip_c)
    d_sum.second()
    arrived(lsb1, lb_sem)
    lsc[...] = lsb[...] + lsb1[...]
    for j in range(3):
        send(lsc, lsc2.at[j], lc_sem + j, line[j])
    dy = d_sum.third().astype(BF16).astype(F32)
    dx_sem = sems()
    for h in range(2):
        back = dot(mix[h], dy[:, h * 128:(h + 1) * 128], **best)
        dxb[y, zl, :, pl.ds(h * 128, 128)] = (dtc[:, h:h + 1] * back).astype(BF16)
    send(dxb.at[y, zl], dxb.at[y, zl], dx_sem, flip_zl)
    dx_ring.start([0])
    for j in range(3):
        arrived(lsc2.at[j], lc_sem + j)
    lring[y] = lsc[...] + lsc2[0] + lsc2[1] + lsc2[2]
    arrived(dxb.at[y, 1 - zl], dx_sem)
    dx_ring.start([1])
    loss_ring.start()
    arrived(hg.at[1 - c], hc_sem)

    def g_block(i, first=False):
        grads = jnp.concatenate([dxb[i, 0], dxb[i, 1]], axis=0)
        for b in range(2):
            tokens = jnp.concatenate([hg[b, 8 + i], hg[b, i]], axis=1)
            rows = pl.ds(b * 256, 256)
            if first:
                gx_ref[rows, :] = dot(tokens, grads)
            else:
                gx_ref[rows, :] += dot(tokens, grads)

    g_block(y, True)
    for k in range(4):
        dx_ring.step(k)
        loss_ring.step(k)
        g_block(lax.rem(y + 7 - k, 8))
        if k < 3:
            g_block(lax.rem(y + k + 1, 8))
    total = jnp.sum(jnp.sum(lring[...], axis=0), axis=0, keepdims=True)
    total = jnp.sum(total, axis=1, keepdims=True) / (TOKENS * WIDTH)
    loss_ref[...] = total

    for copy in pending:
        copy.wait_send()
    for copy, here in lo_copies:
        @pl.when(jnp.logical_not(here))
        def _():
            copy.wait_send()
    for k in range(2):
        from_dp, from_tn = lo_source(k)
        here = (from_dp == dp) & (from_tn == tn)

        @pl.when(jnp.logical_not(here))
        def _():
            arrived(lo_ref.at[:, pl.ds(k * 128, 128)], lo_sem + k)


def store(lo_in, gx_in, loss_in, lo_out, gx_out, loss_out, lo, gx, loss, sem):
    trips = ((gx_in, gx, gx_out), (lo_in, lo, lo_out), (loss_in, loss, loss_out))
    reads = [pltpu.make_async_copy(a, b, sem.at[i]) for i, (a, b, _) in enumerate(trips)]
    writes = [pltpu.make_async_copy(b, d, sem.at[3 + i]) for i, (_, b, d) in enumerate(trips)]
    for move in reads:
        move.start()
    for read, write in zip(reads, writes):
        read.wait()
        write.start()
    for move in writes:
        move.wait()


def local(
    hidden, target, segments, head_map, decay_rate, dt_weight,
    teacher_query, teacher_key, teacher_value, teacher_out,
):
    steps = dt_weight.T
    anywhere = pl.BlockSpec(memory_space=pltpu.HBM)
    vmem = pl.BlockSpec(memory_space=pltpu.VMEM)
    smem = pl.BlockSpec(memory_space=pltpu.SMEM)

    def b(*shape):
        return pltpu.VMEM(shape, BF16)

    def f(*shape):
        return pltpu.VMEM(shape, F32)

    scratch = [
        b(128, 8192), b(2, 128, 128), b(8, 128, 1024), b(8, 128, 256), b(1024, 1024),
        f(8, 16, 128), b(2, 128, 1024), b(128, 1024), b(256, 128), b(2, 16, 256, 128),
        f(256, 256), b(2, 64, 256), b(2, 64, 256), f(2, 64, 256), b(2, 64, 256), b(3, 64, 256),
        b(2, 8, 64, 256),
        f(4, 256, 256), b(2, 2, 128, 256), b(2, 2, 128, 256), b(2, 2, 128, 256), b(3, 128, 256),
        f(16, 8192), f(2, 128, 128), f(128, 16), b(2, 2, 2, 128, 256), b(256, 1024),
        b(4, 2, 256, 128), b(2, 3, 256, 128), f(2, 256, 128), b(256, 128),
        b(256, 128), b(2, 128, 128),
        b(256, 1024), f(4, 256, 256), b(2, 2, 128, 256), b(2, 2, 128, 256),
        b(2, 2, 128, 256), b(3, 128, 256), b(8, 2, 128, 256),
        f(8, 8, 128), f(8, 128), f(8, 128), f(8, 128), f(3, 8, 128), f(8, 8, 128),
        pltpu.SemaphoreType.DMA((N_SEM,)), pltpu.SemaphoreType.DMA((N_SEM,)),
        pltpu.SemaphoreType.DMA((6,)),
    ]
    layer_out, grad_x, loss = pl.pallas_call(
        kernel,
        out_shape=(
            jax.ShapeDtypeStruct((128, 256), BF16),
            jax.ShapeDtypeStruct((512, 256), F32),
            jax.ShapeDtypeStruct((1, 1), F32),
        ),
        in_specs=[anywhere, anywhere, vmem, smem, smem, vmem] + [anywhere] * 4,
        out_specs=(vmem, vmem, vmem),
        scratch_shapes=scratch,
        compiler_params=pltpu.CompilerParams(
            collective_id=0, has_side_effects=True, vmem_limit_bytes=65536 * 1024 - 640 * 1024
        ),
    )(
        hidden, target, segments, head_map, decay_rate, steps,
        teacher_query[0], teacher_key[0], teacher_value[0], teacher_out[0],
    )
    layer_out, grad_x, loss = pl.pallas_call(
        store,
        out_shape=(
            jax.ShapeDtypeStruct((128, 256), BF16),
            jax.ShapeDtypeStruct((512, 256), F32),
            jax.ShapeDtypeStruct((1, 1), F32),
        ),
        in_specs=[anywhere] * 3,
        out_specs=(anywhere,) * 3,
        scratch_shapes=[
            b(128, 256), f(512, 256), f(1, 1), pltpu.SemaphoreType.DMA((6,)),
        ],
    )(layer_out, grad_x, loss)
    return layer_out, grad_x, loss[0, 0]


def solution(mesh):
    in_specs = (
        P("dp", None),
        P("dp", None),
        P("dp", None),
        P("tensor"),
        P("tensor"),
        P("dp", "tensor"),
        P("tensor", "dp", None),
        P("tensor", "dp", None),
        P("tensor", "dp", None),
        P("tensor", None, "dp"),
    )
    out_specs = (P("dp", "tensor"), P("dp", "tensor"), P())
    return jax.shard_map(local, mesh=mesh, in_specs=in_specs, out_specs=out_specs, check_vma=False)
```

```python
import jax
import jax.numpy as jnp
from jax import lax
from jax.experimental import pallas as pl
from jax.experimental.pallas import tpu as pltpu
from jax.sharding import PartitionSpec as P

F32 = jnp.float32
BF16 = jnp.bfloat16
MESH = pl.DeviceIdType.MESH
TOK = 128
TOKENS = 2048
WIDTH = 8192
NY = 8
N_SEM = 192


def dot(a, b, **kw):
    return jnp.dot(a, b, preferred_element_type=F32, **kw)


def dot_t(a, b, **kw):
    return lax.dot_general(a, b, (((1,), (1,)), ((), ())), preferred_element_type=F32, **kw)


def kernel(
    hid_any, tgt_any, seg_ref, map_ref, rate_ref, dtw_ref, q_any, k_any, v_any, o_any,
    lo_ref, gx_ref, loss_ref,
    hid, tg, qg, kvg, og, dtb, hx, hs, ht, hg,
    kvacc, kvp, kvr1, kvt, kvs, kvr2, kvall,
    cacc, cp1, cr1, cp2, cr2,
    w2, mix, dtc, yb, ycat,
    lp, lr1, lt, ls, lr2, lob,
    gob, dacc, dp1, dr1, dp2, dr2, dxb,
    lsa, lsb, lsb1, lsc, lsc2, lring,
    ssem, rsem, lsem,
):
    dp = lax.axis_index("dp")
    tn = lax.axis_index("tensor")
    zl, y = lax.div(dp, 8), lax.rem(dp, 8)
    x, zh, c = lax.div(tn, 8), lax.rem(lax.div(tn, 2), 4), lax.rem(tn, 2)
    zh1, zh0 = lax.div(zh, 2), lax.rem(zh, 2)
    s, q = lax.div(tn, 4), lax.rem(tn, 4)

    def dev(zl_=zl, y_=y, x_=x, zh1_=zh1, zh0_=zh0, c_=c):
        return (zl_ * 8 + y_, x_ * 8 + zh1_ * 4 + zh0_ * 2 + c_)

    def s_dev(s_):
        return dev(x_=lax.div(s_, 2), zh1_=lax.rem(s_, 2))

    flip_zl, flip_c, flip_h = dev(zl_=1 - zl), dev(c_=1 - c), dev(zh0_=1 - zh0)
    flip_zh = dev(zl_=1 - zl, zh0_=1 - zh0)
    flip_h1 = dev(zh1_=1 - zh1)
    line = (flip_h, flip_zl, flip_zh)

    count = [0]
    pending = []

    def sems(n=1):
        first = count[0]
        count[0] += n
        return first

    def rcopy(src, dst, i, target):
        return pltpu.make_async_remote_copy(
            src_ref=src, dst_ref=dst, send_sem=ssem.at[i], recv_sem=rsem.at[i],
            device_id=target, device_id_type=MESH,
        )

    def send(src, dst, i, target):
        copy = rcopy(src, dst, i, target)
        copy.start()
        pending.append(copy)

    def arrived(dst, i):
        rcopy(dst, dst, i, flip_c).wait_recv()

    def column(index):
        return pl.ds(pl.multiple_of(index * 128, 128), 128)

    def stage(src, dst, i):
        copy = pltpu.make_async_copy(src, dst, lsem.at[i])
        copy.start()
        return copy

    lo_t = lax.div(tn, 16)
    lo_s = lax.div(lax.rem(tn, 16), 2)
    lo_q = 2 * lax.rem(tn, 2)

    def lo_source(slot):
        return (lo_t * 8 + y, lo_s * 4 + lo_q + slot)

    perm_from = (lax.rem(lax.div(tn, 2) + 8, 16), 2 * dp + c)
    perm_to = (lax.div(tn, 2), 2 * lax.rem(dp + 8, 16) + c)
    greeted = [dev(y_=lax.rem(y + 1, 8)), dev(y_=lax.rem(y + 7, 8))]
    greeted += [flip_zl, flip_c, flip_h, flip_zh]
    greeted += [s_dev(lax.rem(s + d, 8)) for d in range(1, 8)]

    def zh_dev(d):
        other = lax.rem(zh + d, 4)
        return dev(zh1_=lax.div(other, 2), zh0_=lax.rem(other, 2))

    def x_dev(d):
        return dev(x_=lax.rem(x + d, 4))

    greeted += [zh_dev(d) for d in range(1, 4)]
    greeted += [perm_from, lo_source(0), lo_source(1)]
    barrier = pltpu.get_barrier_semaphore()
    for target in greeted:
        pl.semaphore_signal(barrier, inc=1, device_id=target, device_id_type=MESH)

    hid_in = stage(hid_any, hid, 0)
    key_in = stage(k_any, kvg.at[y, :, pl.ds(0, 128)], 1)
    value_in = stage(v_any, kvg.at[y, :, pl.ds(128, 128)], 2)
    query_in = stage(q_any, qg.at[y], 3)
    out_in = stage(o_any, og.at[:, column(y)], 4)
    own_target = tgt_any.at[:, column((zl * 8 + s) * 4 + q)]
    target_in = stage(own_target, tg.at[zl], 5)

    key_in.wait()
    value_in.wait()
    query_in.wait()
    pl.semaphore_wait(barrier, len(greeted))

    class Ring:
        def __init__(self, part, chunks):
            self.part, self.chunks = part, chunks
            self.base = sems(8 * chunks)

        def live(self, k, d, ch):
            if k < 3:
                return True
            return d == 0 if self.chunks == 1 else d == ch

        def block(self, k, d):
            return lax.rem(y + (8 - k if d == 0 else k), 8)

        def sem(self, k, d, ch):
            return self.base + (k * 2 + d) * self.chunks + ch

        def send(self, k, d, ch):
            ref = self.part(self.block(k, d), ch)
            to = dev(y_=lax.rem(y + (1 if d == 0 else 7), 8))
            send(ref, ref, self.sem(k, d, ch), to)

        def start(self, chunks=None):
            for ch in range(self.chunks) if chunks is None else chunks:
                for d in range(2):
                    self.send(0, d, ch)

        def step(self, k, chunks=None):
            for ch in range(self.chunks) if chunks is None else chunks:
                for d in range(2):
                    if self.live(k, d, ch):
                        arrived(self.part(self.block(k + 1, d), ch), self.sem(k, d, ch))
                        if k < 3 and self.live(k + 1, d, ch):
                            self.send(k + 1, d, ch)

    kv_ring = Ring(lambda b, ch: kvg.at[b, pl.ds(ch * 64, 64)], 2)
    q_ring = Ring(lambda b, ch: qg.at[b, pl.ds(ch * 64, 64)], 2)
    o_ring = Ring(lambda b, ch: og.at[pl.ds(ch * 512, 512), column(b)], 2)
    dt_ring = Ring(lambda b, ch: dtb.at[b, pl.ds(ch * 8, 8)], 2)
    dx_ring = Ring(lambda b, ch: dxb.at[b, 1 - zl if ch else zl], 2)
    loss_ring = Ring(lambda b, ch: lring.at[b], 1)

    h_sem, t_sem, dt_sem, p_sem = sems(), sems(), sems(), sems()
    kv_ring.start()
    q_ring.start()
    steps = dtw_ref[...].astype(F32)
    for r in range(8):
        lanes = slice((r % 4) * 128, (r % 4 + 1) * 128)
        dtb[y, pl.ds(zl * 8 + r, 1), :] = steps[r // 4:r // 4 + 1, lanes]
    dt_own = dtb.at[y, pl.ds(pl.multiple_of(zl * 8, 8), 8)]
    send(dt_own, dt_own, dt_sem, flip_zl)
    hid_in.wait()
    for i in range(NY):
        hs[:, pl.ds(i * 128, 128)] = hid[:, column(((1 - zl) * 8 + i) * 4 + q)]
    send(hs, hx.at[zl], h_sem, flip_zl)
    kv_ring.step(0)
    tile = hid[:, pl.ds(pl.multiple_of(tn * 256, 256), 256)]
    ht[...] = tile.astype(F32).T.astype(BF16)
    send(ht, hg.at[c, lax.rem(dp + 8, 16)], p_sem, perm_to)
    for i in range(NY):
        hx[zl, :, pl.ds(i * 128, 128)] = hid[:, column((zl * 8 + i) * 4 + q)]
    q_ring.step(0, [0])
    kv_ring.step(1)
    q_ring.step(0, [1])

    def rows_of(i):
        lanes = column(i)
        pieces = [hx[zz, pl.ds(hf * 64, 64), lanes] for hf in range(2) for zz in range(2)]
        return jnp.concatenate(pieces, axis=0)

    def q_add(j, value, fresh=False):
        for hf in range(2):
            half = value[hf * 128:(hf + 1) * 128]
            cacc[hf, j] = half if fresh else cacc[hf, j] + half

    def q_pair(k):
        up, down = lax.rem(y + k, 8), lax.rem(y + 8 - k, 8)
        rows_up, rows_down = rows_of(up), rows_of(down)
        for j in range(4):
            lanes = pl.ds(j * 256, 256)
            q_add(j, dot(rows_up, qg[up, :, lanes]) + dot(rows_down, qg[down, :, lanes]))

    arrived(hx.at[1 - zl], h_sem)
    arrived(dtb.at[y, pl.ds(pl.multiple_of((1 - zl) * 8, 8), 8)], dt_sem)
    dt_ring.start()
    other_target = tgt_any.at[:, column(((1 - zl) * 8 + s) * 4 + q)]
    send(other_target, tg.at[zl], t_sem, flip_zl)
    rows = rows_of(y)
    for j in range(4):
        q_add(j, dot(rows, qg[y, :, pl.ds(j * 256, 256)]), True)
    q_ring.step(1, [0])
    kv_ring.step(2)
    q_ring.step(1, [1])
    hz_sem = sems(3)
    own_tile = hg.at[c, lax.div(tn, 2)]
    arrived(own_tile, p_sem)
    for d in range(1, 4):
        send(own_tile, own_tile, hz_sem + d - 1, zh_dev(d))
    q_pair(1)
    dt_ring.step(0)
    out_in.wait()
    q_ring.step(2, [0])
    kv_ring.step(3)
    k1_sem, k2_sem, k3_sem, k4_sem = sems(), sems(3), sems(7), sems()
    rows = jnp.concatenate([hx[0], hx[1]], axis=0)
    kvacc[...] = dot(rows, kvg[...].reshape(1024, 256))
    for zz in range(2):
        kvp[zz] = kvacc[pl.ds(pl.multiple_of(zz * 128 + (1 - c) * 64, 64), 64), :].astype(BF16)
    send(kvp, kvr1, k1_sem, flip_c)
    q_ring.step(2, [1])
    o_ring.start()
    dt_ring.step(1)
    arrived(kvr1, k1_sem)
    for zz in range(2):
        part = kvacc[pl.ds(pl.multiple_of(zz * 128 + c * 64, 64), 64), :] + kvr1[zz].astype(F32)
        kvt[zz] = part
        kvs[zz] = part.astype(BF16)
    send(kvs.at[1 - zl], kvr2.at[2], k2_sem + 2, flip_zh)
    send(kvs.at[zl], kvr2.at[0], k2_sem, flip_h)
    send(kvs.at[1 - zl], kvr2.at[1], k2_sem + 1, flip_zl)
    hx_sem = sems(3)
    for d in range(1, 4):
        arrived(hg.at[c, x * 4 + lax.rem(zh + 4 - d, 4)], hz_sem + d - 1)
    quad = hg.at[c, pl.ds(x * 4, 4)]
    for d in range(1, 4):
        send(quad, quad, hx_sem + d - 1, x_dev(d))
    q_pair(2)
    dt_ring.step(2)
    q_ring.step(3)
    for j in range(3):
        arrived(kvr2.at[j], k2_sem + j)
    kvall[c, s] = (
        kvt[zl] + kvr2[0].astype(F32) + kvr2[1].astype(F32) + kvr2[2].astype(F32)
    ).astype(BF16)
    own_kv = kvall.at[c, s]
    for d in (1, 3, 5, 7, 2, 4, 6):
        send(own_kv, own_kv, k3_sem + d - 1, s_dev(lax.rem(s + d, 8)))

    class Sum8:
        def __init__(self, acc, p1, r1, p2, r2, rows):
            self.acc, self.p1, self.r1, self.p2, self.r2 = acc, p1, r1, p2, r2
            self.rows = rows
            self.s1, self.s2 = sems(), sems(3)

        def first(self, add, fresh=False):
            n = self.rows
            for hh in range(2):
                part = add(hh * 2 + 1 - c)
                if not fresh:
                    part += self.acc[hh * 2 + 1 - c]
                for zz in range(2):
                    self.p1[zz, hh] = part[zz * n:(zz + 1) * n].astype(BF16)
            send(self.p1, self.r1, self.s1, flip_c)
            for hh in range(2):
                if fresh:
                    self.acc[hh * 2 + c] = add(hh * 2 + c)
                else:
                    self.acc[hh * 2 + c] += add(hh * 2 + c)

        def second(self):
            n = self.rows
            arrived(self.r1, self.s1)
            for zz in range(2):
                for hh in range(2):
                    rows = pl.ds(zz * n, n)
                    part = self.acc[hh * 2 + c, rows, :] + self.r1[zz, hh].astype(F32)
                    self.acc[hh * 2 + c, rows, :] = part
                    self.p2[zz, hh] = part.astype(BF16)
            send(self.p2.at[1 - zl, 1 - zh0], self.r2.at[2], self.s2 + 2, flip_zh)
            send(self.p2.at[zl, 1 - zh0], self.r2.at[0], self.s2, flip_h)
            send(self.p2.at[1 - zl, zh0], self.r2.at[1], self.s2 + 1, flip_zl)

        def third(self):
            n = self.rows
            for j in range(3):
                arrived(self.r2.at[j], self.s2 + j)
            own = self.acc[zh0 * 2 + c, pl.ds(pl.multiple_of(zl * n, n), n), :]
            return own + self.r2[0].astype(F32) + self.r2[1].astype(F32) + self.r2[2].astype(F32)

    c_sums = [
        Sum8(cacc.at[hf], cp1.at[hf], cr1.at[hf], cp2.at[hf], cr2.at[hf], 64) for hf in range(2)
    ]

    last = [lax.rem(y + k, 8) for k in (3, 4, 5)]
    last_rows = [rows_of(i) for i in last]
    for hf in range(2):

        def last_q(k):
            lanes = pl.ds(pl.multiple_of(k * 256, 256), 256)
            rows = slice(hf * 128, (hf + 1) * 128)
            return sum(dot(r[rows], qg[i, :, lanes]) for r, i in zip(last_rows, last))

        c_sums[hf].first(last_q)
    o_ring.step(0, [0])
    c_sums[0].second()
    c_sums[1].second()
    dt_ring.step(3)
    o_ring.step(0, [1])
    w2[...] = jnp.zeros_like(w2)
    for m in range(16):
        for j in range(4):
            for h in range(2):
                w2[h:h + 1, pl.ds((m * 4 + j) * 128, 128)] = dtb[
                    m % 8, pl.ds((m // 8) * 8 + h * 4 + j, 1), :
                ]

    o_ring.step(1, [0])
    best = dict(precision=lax.Precision.HIGHEST)
    weights = w2[...].astype(BF16)

    def softplus(v):
        return jnp.maximum(v, 0.0) + jnp.log1p(jnp.exp(-jnp.abs(v)))

    step_col = softplus(dot_t(hid[...], weights))
    step_row = softplus(dot_t(weights, hid[...]))
    dtc[...] = step_col
    rate0, rate1 = rate_ref[0], rate_ref[1]
    n_lane = step_col.shape[1]
    lane = lax.broadcasted_iota(jnp.int32, (TOK, n_lane), 1)
    subl = lax.broadcasted_iota(jnp.int32, (n_lane, TOK), 0)
    at_t = lax.broadcasted_iota(jnp.int32, (TOK, TOK), 0)
    at_j = lax.broadcasted_iota(jnp.int32, (TOK, TOK), 1)
    lower = (at_j <= at_t).astype(F32)
    upper = (at_t <= at_j).astype(F32)
    cs_col = dot(lower, step_col * jnp.where(lane == 0, rate0, rate1), **best)
    cs_row = dot(step_row * jnp.where(subl == 0, rate0, rate1), upper, **best)
    seg_row = jnp.broadcast_to(seg_ref[...].astype(F32), (TOK, TOK))
    visible = (seg_row == seg_row.T) & (at_j <= at_t)
    for h in range(2):
        distance = jnp.where(visible, cs_col[:, h:h + 1] - cs_row[h:h + 1, :], 0.0)
        mix[h] = jnp.where(visible, jnp.exp(-distance), 0.0)

    o_ring.step(1, [1])
    for d in range(1, 8):
        arrived(kvall.at[c, lax.rem(s + 8 - d, 8)], k3_sem + d - 1)
    send(kvall.at[c], kvall.at[c], k4_sem, flip_c)
    y_sem, y2_sem = sems(6), sems(2)
    arrived(kvall.at[1 - c], k4_sem)
    keys, sources = [], []
    for h in range(2):
        head = map_ref[h]
        both = jnp.concatenate([kvall[0, head], kvall[1, head]], axis=0)
        keys.append(both[:, :128])
        sources.append(dtc[:, h:h + 1] * both[:, 128:].astype(F32))

    def y_rows(hf, zz, hh):
        return yb.at[c, zz, hh, pl.ds(hf * 64, 64)]

    for hf in range(2):
        rows = pl.ds(hf * 64, 64)
        c_half = (c_sums[hf].third() * (128 ** -0.5)).astype(BF16)
        for h in range(2):
            lanes = slice(h * 128, (h + 1) * 128)
            mixing = dot_t(c_half[:, lanes], keys[h]) * mix[h, rows]
            mix[h, rows] = mixing
            yb[c, zl, zh0, rows, pl.ds(h * 128, 128)] = dot(
                mixing, sources[h], **best
            ).astype(BF16)
        own_y = y_rows(hf, zl, zh0)
        send(own_y, own_y, y_sem + hf * 3 + 2, flip_zh)
        send(own_y, own_y, y_sem + hf * 3, flip_h)
        send(own_y, own_y, y_sem + hf * 3 + 1, flip_zl)
    for h in range(2):
        mix[h] = mix[h].T
    o_ring.step(2)
    for hf in range(2):
        arrived(y_rows(hf, zl, 1 - zh0), y_sem + hf * 3)
        arrived(y_rows(hf, 1 - zl, zh0), y_sem + hf * 3 + 1)
        arrived(y_rows(hf, 1 - zl, 1 - zh0), y_sem + hf * 3 + 2)
        both_y = yb.at[c, :, :, pl.ds(hf * 64, 64)]
        send(both_y, both_y, y2_sem + hf, flip_c)
    hc_sem = sems()
    o_ring.step(3)

    def y_all(hf):
        arrived(yb.at[1 - c, :, :, pl.ds(hf * 64, 64)], y2_sem + hf)
        for zz in range(2):
            for hh in range(2):
                for cc in range(2):
                    rows = pl.ds(hf * 128 + zz * 64, 64)
                    lanes = pl.ds((hh * 2 + cc) * 256, 256)
                    ycat[rows, lanes] = yb[cc, zz, hh, pl.ds(hf * 64, 64)]

    halves = range(2)
    l0_sem, l1_sem, l2_sem = sems(6), sems(6), sems(2)
    for hf in halves:
        y_all(hf)
        for d in (2, 1, 3, 0):
            at = lax.rem(x + d, 4)
            lanes = pl.ds(pl.multiple_of(at * 256, 256), 256)
            value = dot(ycat[pl.ds(hf * 128, 128), :], og[:, lanes])
            if d:
                i = hf * 3 + d - 1
                lp[hf, at, 0] = value[:, :128].astype(BF16)
                lp[hf, at, 1] = value[:, 128:].astype(BF16)
                send(lp.at[hf, at, 1 - zh1], lr1.at[hf, 1, d - 1], l0_sem + i, x_dev(d))
            else:
                lt[hf, 0] = value[:, :128]
                lt[hf, 1] = value[:, 128:]
    for hf in halves:
        for d in (2, 1, 3):
            at = lax.rem(x + d, 4)
            send(lp.at[hf, at, zh1], lr1.at[hf, 0, d - 1], l1_sem + hf * 3 + d - 1, x_dev(d))
    for hf in halves:
        part = lt[hf, 1 - zh1]
        for d in range(3):
            arrived(lr1.at[hf, 1, d], l0_sem + hf * 3 + d)
            part += lr1[hf, 1, d].astype(F32)
        ls[hf] = part.astype(BF16)
        send(ls.at[hf], lr2.at[hf], l2_sem + hf, flip_h1)
    for d in range(1, 4):
        arrived(hg.at[c, pl.ds(lax.rem(x + 4 - d, 4) * 4, 4)], hx_sem + d - 1)
    send(hg.at[c], hg.at[c], hc_sem, flip_c)
    target_in.wait()
    arrived(tg.at[1 - zl], t_sem)
    g1_sem, g2_sem, g3_sem, la_sem, la2_sem = sems(2), sems(6), sems(6), sems(), sems(3)
    squares = jnp.zeros((8, 128), F32)

    def g_piece(hf, index):
        return gob.at[pl.ds(hf * 128, 128), column(index)]

    for hf in halves:
        part = lt[hf, zh1]
        for d in range(3):
            arrived(lr1.at[hf, 0, d], l1_sem + hf * 3 + d)
            part += lr1[hf, 0, d].astype(F32)
        arrived(lr2.at[hf], l2_sem + hf)
        layer = (part + lr2[hf].astype(F32)).astype(BF16)
        for zz in range(2):
            rows = layer[zz * 64:(zz + 1) * 64]
            lob[zz, pl.ds(hf * 64, 64)] = rows
            residual = rows.astype(F32) - tg[zz, pl.ds(hf * 64, 64)].astype(F32)
            gob[pl.ds(hf * 128 + zz * 64, 64), column(s)] = (2.0 * residual / TOKENS).astype(BF16)
            squares += jnp.sum((residual * residual).reshape(8, 8, 128), axis=0)
        own_g = g_piece(hf, s)
        send(own_g, own_g, g1_sem + hf, flip_h1)
        for d in (2, 1, 3):
            send(own_g, own_g, g2_sem + hf * 3 + d - 1, x_dev(d))
    lsa[s] = squares
    send(lsa.at[s], lsa.at[s], la_sem, flip_h1)
    for hf in halves:
        next_g = g_piece(hf, 2 * x + 1 - zh1)
        arrived(next_g, g1_sem + hf)
        for d in (2, 1, 3):
            send(next_g, next_g, g3_sem + hf * 3 + d - 1, x_dev(d))

    lo_sem = sems(2)
    lo_tn = 16 * zl + 2 * s + lax.div(q, 2)
    slot = lax.rem(q, 2)
    lo_dst = lo_ref.at[:, column(slot)]
    lo_copies = []
    for zz in range(2):
        to = (zz * 8 + y, lo_tn)
        here = (zl == zz) & (lo_tn == tn)
        copy = pltpu.make_async_remote_copy(
            src_ref=lob.at[zz], dst_ref=lo_dst, send_sem=ssem.at[lo_sem + zz],
            recv_sem=rsem.at[lo_sem + slot], device_id=to, device_id_type=MESH,
        )
        lo_copies.append((copy, here))

        @pl.when(here)
        def _():
            lo_ref[:, column(slot)] = lob[zz]

        @pl.when(jnp.logical_not(here))
        def _():
            copy.start()

    arrived(lsa.at[2 * x + 1 - zh1], la_sem)
    loss_pair = lsa.at[pl.ds(x * 2, 2)]
    for d in range(1, 4):
        send(loss_pair, loss_pair, la2_sem + d - 1, x_dev(d))
    d_sums = [
        Sum8(dacc.at[hf], dp1.at[hf], dr1.at[hf], dp2.at[hf], dr2.at[hf], 64) for hf in halves
    ]
    for hf in halves:
        for d in (1, 3, 2):
            at = lax.rem(x + 4 - d, 4)
            arrived(g_piece(hf, at * 2 + zh1), g2_sem + hf * 3 + d - 1)
            arrived(g_piece(hf, at * 2 + 1 - zh1), g3_sem + hf * 3 + d - 1)
        rows = gob[pl.ds(hf * 128, 128), :]

        def part(k):
            return dot_t(rows, og[pl.ds(pl.multiple_of(k * 256, 256), 256), :])

        d_sums[hf].first(part, True)
        if hf:
            d_sums[0].second()
    d_sums[1].second()
    lb_sem, lc_sem = sems(), sems(3)
    for d in range(1, 4):
        arrived(lsa.at[pl.ds(lax.rem(x + 4 - d, 4) * 2, 2)], la2_sem + d - 1)
    total = lsa[0]
    for i in range(1, 8):
        total += lsa[i]
    lsb[...] = total
    send(lsb, lsb1, lb_sem, flip_c)
    arrived(lsb1, lb_sem)
    lsc[...] = lsb[...] + lsb1[...]
    for j in range(3):
        send(lsc, lsc2.at[j], lc_sem + j, line[j])
    dy = jnp.concatenate([d_sums[hf].third() for hf in halves], axis=0)
    dy = dy.astype(BF16).astype(F32)
    dx_sem = sems()
    for h in range(2):
        back = dot(mix[h], dy[:, h * 128:(h + 1) * 128], **best)
        dxb[y, zl, :, pl.ds(h * 128, 128)] = (dtc[:, h:h + 1] * back).astype(BF16)
    send(dxb.at[y, zl], dxb.at[y, zl], dx_sem, flip_zl)
    dx_ring.start([0])
    for j in range(3):
        arrived(lsc2.at[j], lc_sem + j)
    lring[y] = lsc[...] + lsc2[0] + lsc2[1] + lsc2[2]
    arrived(dxb.at[y, 1 - zl], dx_sem)
    dx_ring.start([1])
    loss_ring.start()
    arrived(hg.at[1 - c], hc_sem)

    def g_block(i, first=False):
        grads = jnp.concatenate([dxb[i, 0], dxb[i, 1]], axis=0)
        for b in range(2):
            tokens = jnp.concatenate([hg[b, 8 + i], hg[b, i]], axis=1)
            rows = pl.ds(b * 256, 256)
            if first:
                gx_ref[rows, :] = dot(tokens, grads)
            else:
                gx_ref[rows, :] += dot(tokens, grads)

    g_block(y, True)
    for k in range(4):
        dx_ring.step(k)
        loss_ring.step(k)
        g_block(lax.rem(y + 7 - k, 8))
        if k < 3:
            g_block(lax.rem(y + k + 1, 8))
    total = jnp.sum(jnp.sum(lring[...], axis=0), axis=0, keepdims=True)
    total = jnp.sum(total, axis=1, keepdims=True) / (TOKENS * WIDTH)
    loss_ref[...] = total

    for copy in pending:
        copy.wait_send()
    for copy, here in lo_copies:
        @pl.when(jnp.logical_not(here))
        def _():
            copy.wait_send()
    for k in range(2):
        from_dp, from_tn = lo_source(k)
        here = (from_dp == dp) & (from_tn == tn)

        @pl.when(jnp.logical_not(here))
        def _():
            arrived(lo_ref.at[:, pl.ds(k * 128, 128)], lo_sem + k)


def store(lo_in, gx_in, loss_in, lo_out, gx_out, loss_out, lo, gx, loss, sem):
    trips = ((gx_in, gx, gx_out), (lo_in, lo, lo_out), (loss_in, loss, loss_out))
    reads = [pltpu.make_async_copy(a, b, sem.at[i]) for i, (a, b, _) in enumerate(trips)]
    writes = [pltpu.make_async_copy(b, d, sem.at[3 + i]) for i, (_, b, d) in enumerate(trips)]
    for move in reads:
        move.start()
    for read, write in zip(reads, writes):
        read.wait()
        write.start()
    for move in writes:
        move.wait()


def local(
    hidden, target, segments, head_map, decay_rate, dt_weight,
    teacher_query, teacher_key, teacher_value, teacher_out,
):
    steps = dt_weight.T
    anywhere = pl.BlockSpec(memory_space=pltpu.HBM)
    vmem = pl.BlockSpec(memory_space=pltpu.VMEM)
    smem = pl.BlockSpec(memory_space=pltpu.SMEM)

    def b(*shape):
        return pltpu.VMEM(shape, BF16)

    def f(*shape):
        return pltpu.VMEM(shape, F32)

    scratch = [
        b(128, 8192), b(2, 128, 128), b(8, 128, 1024), b(8, 128, 256), b(1024, 1024),
        f(8, 16, 128), b(2, 128, 1024), b(128, 1024), b(256, 128), b(2, 16, 256, 128),
        f(256, 256), b(2, 64, 256), b(2, 64, 256), f(2, 64, 256), b(2, 64, 256), b(3, 64, 256),
        b(2, 8, 64, 256),
        f(2, 4, 128, 256), b(2, 2, 2, 64, 256), b(2, 2, 2, 64, 256), b(2, 2, 2, 64, 256),
        b(2, 3, 64, 256),
        f(16, 8192), f(2, 128, 128), f(128, 16), b(2, 2, 2, 128, 256), b(256, 1024),
        b(2, 4, 2, 128, 128), b(2, 2, 3, 128, 128), f(2, 2, 128, 128), b(2, 128, 128),
        b(2, 128, 128), b(2, 128, 128),
        b(256, 1024), f(2, 4, 128, 256), b(2, 2, 2, 64, 256), b(2, 2, 2, 64, 256),
        b(2, 2, 2, 64, 256), b(2, 3, 64, 256), b(8, 2, 128, 256),
        f(8, 8, 128), f(8, 128), f(8, 128), f(8, 128), f(3, 8, 128), f(8, 8, 128),
        pltpu.SemaphoreType.DMA((N_SEM,)), pltpu.SemaphoreType.DMA((N_SEM,)),
        pltpu.SemaphoreType.DMA((6,)),
    ]
    layer_out, grad_x, loss = pl.pallas_call(
        kernel,
        out_shape=(
            jax.ShapeDtypeStruct((128, 256), BF16),
            jax.ShapeDtypeStruct((512, 256), F32),
            jax.ShapeDtypeStruct((1, 1), F32),
        ),
        in_specs=[anywhere, anywhere, vmem, smem, smem, vmem] + [anywhere] * 4,
        out_specs=(vmem, vmem, vmem),
        scratch_shapes=scratch,
        compiler_params=pltpu.CompilerParams(
            collective_id=0, has_side_effects=True, vmem_limit_bytes=65536 * 1024 - 640 * 1024
        ),
    )(
        hidden, target, segments, head_map, decay_rate, steps,
        teacher_query[0], teacher_key[0], teacher_value[0], teacher_out[0],
    )
    layer_out, grad_x, loss = pl.pallas_call(
        store,
        out_shape=(
            jax.ShapeDtypeStruct((128, 256), BF16),
            jax.ShapeDtypeStruct((512, 256), F32),
            jax.ShapeDtypeStruct((1, 1), F32),
        ),
        in_specs=[anywhere] * 3,
        out_specs=(anywhere,) * 3,
        scratch_shapes=[
            b(128, 256), f(512, 256), f(1, 1), pltpu.SemaphoreType.DMA((6,)),
        ],
    )(layer_out, grad_x, loss)
    return layer_out, grad_x, loss[0, 0]


def solution(mesh):
    in_specs = (
        P("dp", None),
        P("dp", None),
        P("dp", None),
        P("tensor"),
        P("tensor"),
        P("dp", "tensor"),
        P("tensor", "dp", None),
        P("tensor", "dp", None),
        P("tensor", "dp", None),
        P("tensor", None, "dp"),
    )
    out_specs = (P("dp", "tensor"), P("dp", "tensor"), P())
    return jax.shard_map(local, mesh=mesh, in_specs=in_specs, out_specs=out_specs, check_vma=False)
```

```python
import jax
import jax.numpy as jnp
from jax import lax
from jax.experimental import pallas as pl
from jax.experimental.pallas import tpu as pltpu
from jax.sharding import PartitionSpec as P

F32 = jnp.float32
BF16 = jnp.bfloat16
MESH = pl.DeviceIdType.MESH
TOK = 128
TOKENS = 2048
WIDTH = 8192
NY = 8
N_SEM = 192


def dot(a, b, **kw):
    return jnp.dot(a, b, preferred_element_type=F32, **kw)


def dot_t(a, b, **kw):
    return lax.dot_general(a, b, (((1,), (1,)), ((), ())), preferred_element_type=F32, **kw)


def kernel(
    hid_any, tgt_any, seg_ref, map_ref, rate_ref, dtw_ref, q_any, k_any, v_any, o_any,
    lo_ref, gx_ref, loss_ref,
    hid, tg, qg, kvg, og, dtb, hx, hs, ht, hg,
    kvacc, kvp, kvr1, kvt, kvs, kvr2, kvall,
    cacc, cp1, cr1, cp2, cr2,
    w2, mix, dtc, yb, ycat,
    lp, lr1, lt, ls, lr2, lob,
    gob, dacc, dp1, dr1, dp2, dr2, dxb,
    lsa, lsb, lsb1, lsc, lsc2, lring,
    ssem, rsem, lsem,
):
    dp = lax.axis_index("dp")
    tn = lax.axis_index("tensor")
    zl, y = lax.div(dp, 8), lax.rem(dp, 8)
    x, zh, c = lax.div(tn, 8), lax.rem(lax.div(tn, 2), 4), lax.rem(tn, 2)
    zh1, zh0 = lax.div(zh, 2), lax.rem(zh, 2)
    s, q = lax.div(tn, 4), lax.rem(tn, 4)

    def dev(zl_=zl, y_=y, x_=x, zh1_=zh1, zh0_=zh0, c_=c):
        return (zl_ * 8 + y_, x_ * 8 + zh1_ * 4 + zh0_ * 2 + c_)

    def s_dev(s_):
        return dev(x_=lax.div(s_, 2), zh1_=lax.rem(s_, 2))

    flip_zl, flip_c, flip_h = dev(zl_=1 - zl), dev(c_=1 - c), dev(zh0_=1 - zh0)
    flip_zh = dev(zl_=1 - zl, zh0_=1 - zh0)
    flip_h1 = dev(zh1_=1 - zh1)
    line = (flip_h, flip_zl, flip_zh)

    count = [0]
    pending = []

    def sems(n=1):
        first = count[0]
        count[0] += n
        return first

    def rcopy(src, dst, i, target):
        return pltpu.make_async_remote_copy(
            src_ref=src, dst_ref=dst, send_sem=ssem.at[i], recv_sem=rsem.at[i],
            device_id=target, device_id_type=MESH,
        )

    def send(src, dst, i, target):
        copy = rcopy(src, dst, i, target)
        copy.start()
        pending.append(copy)

    def arrived(dst, i):
        rcopy(dst, dst, i, flip_c).wait_recv()

    def column(index):
        return pl.ds(pl.multiple_of(index * 128, 128), 128)

    def stage(src, dst, i):
        copy = pltpu.make_async_copy(src, dst, lsem.at[i])
        copy.start()
        return copy

    lo_t = lax.div(tn, 16)
    lo_s = lax.div(lax.rem(tn, 16), 2)
    lo_q = 2 * lax.rem(tn, 2)

    def lo_source(slot):
        return (lo_t * 8 + y, lo_s * 4 + lo_q + slot)

    perm_from = (lax.rem(lax.div(tn, 2) + 8, 16), 2 * dp + c)
    perm_to = (lax.div(tn, 2), 2 * lax.rem(dp + 8, 16) + c)
    greeted = [dev(y_=lax.rem(y + 1, 8)), dev(y_=lax.rem(y + 7, 8))]
    greeted += [flip_zl, flip_c, flip_h, flip_zh]
    greeted += [s_dev(lax.rem(s + d, 8)) for d in range(1, 8)]

    def zh_dev(d):
        other = lax.rem(zh + d, 4)
        return dev(zh1_=lax.div(other, 2), zh0_=lax.rem(other, 2))

    def x_dev(d):
        return dev(x_=lax.rem(x + d, 4))

    greeted += [zh_dev(d) for d in range(1, 4)]
    greeted += [perm_from, lo_source(0), lo_source(1)]
    barrier = pltpu.get_barrier_semaphore()
    for target in greeted:
        pl.semaphore_signal(barrier, inc=1, device_id=target, device_id_type=MESH)

    hid_in = stage(hid_any, hid, 0)
    key_in = stage(k_any, kvg.at[y, :, pl.ds(0, 128)], 1)
    value_in = stage(v_any, kvg.at[y, :, pl.ds(128, 128)], 2)
    query_in = stage(q_any, qg.at[y], 3)
    out_in = stage(o_any, og.at[:, column(y)], 4)
    own_target = tgt_any.at[:, column((zl * 8 + s) * 4 + q)]
    target_in = stage(own_target, tg.at[zl], 5)

    key_in.wait()
    value_in.wait()
    query_in.wait()
    pl.semaphore_wait(barrier, len(greeted))

    class Ring:
        def __init__(self, part, chunks):
            self.part, self.chunks = part, chunks
            self.base = sems(8 * chunks)

        def live(self, k, d, ch):
            if k < 3:
                return True
            return d == 0 if self.chunks == 1 else d == ch

        def block(self, k, d):
            return lax.rem(y + (8 - k if d == 0 else k), 8)

        def sem(self, k, d, ch):
            return self.base + (k * 2 + d) * self.chunks + ch

        def send(self, k, d, ch):
            ref = self.part(self.block(k, d), ch)
            to = dev(y_=lax.rem(y + (1 if d == 0 else 7), 8))
            send(ref, ref, self.sem(k, d, ch), to)

        def start(self, chunks=None):
            for ch in range(self.chunks) if chunks is None else chunks:
                for d in range(2):
                    self.send(0, d, ch)

        def step(self, k, chunks=None):
            for ch in range(self.chunks) if chunks is None else chunks:
                for d in range(2):
                    if self.live(k, d, ch):
                        arrived(self.part(self.block(k + 1, d), ch), self.sem(k, d, ch))
                        if k < 3 and self.live(k + 1, d, ch):
                            self.send(k + 1, d, ch)

    kv_ring = Ring(lambda b, ch: kvg.at[b], 1)
    q_ring = Ring(lambda b, ch: qg.at[b, pl.ds(ch * 64, 64)], 2)
    o_ring = Ring(lambda b, ch: og.at[pl.ds(ch * 512, 512), column(b)], 2)
    dt_ring = Ring(lambda b, ch: dtb.at[b], 1)
    dx_ring = Ring(lambda b, ch: dxb.at[b, 1 - zl if ch else zl], 2)
    loss_ring = Ring(lambda b, ch: lring.at[b], 1)

    h_sem, t_sem, dt_sem, p_sem = sems(), sems(), sems(), sems()
    kv_ring.start()
    q_ring.start()
    steps = dtw_ref[...].astype(F32)
    for r in range(8):
        lanes = slice((r % 4) * 128, (r % 4 + 1) * 128)
        dtb[y, pl.ds(zl * 8 + r, 1), :] = steps[r // 4:r // 4 + 1, lanes]
    dt_own = dtb.at[y, pl.ds(pl.multiple_of(zl * 8, 8), 8)]
    send(dt_own, dt_own, dt_sem, flip_zl)
    hid_in.wait()
    for i in range(NY):
        hs[:, pl.ds(i * 128, 128)] = hid[:, column(((1 - zl) * 8 + i) * 4 + q)]
    send(hs, hx.at[zl], h_sem, flip_zl)
    kv_ring.step(0)
    tile = hid[:, pl.ds(pl.multiple_of(tn * 256, 256), 256)]
    ht[...] = tile.astype(F32).T.astype(BF16)
    send(ht, hg.at[c, lax.rem(dp + 8, 16)], p_sem, perm_to)
    for i in range(NY):
        hx[zl, :, pl.ds(i * 128, 128)] = hid[:, column((zl * 8 + i) * 4 + q)]
    q_ring.step(0, [0])
    kv_ring.step(1)
    q_ring.step(0, [1])

    def rows_of(i):
        lanes = column(i)
        pieces = [hx[zz, pl.ds(hf * 64, 64), lanes] for hf in range(2) for zz in range(2)]
        return jnp.concatenate(pieces, axis=0)

    def q_add(j, value, fresh=False):
        for hf in range(2):
            half = value[hf * 128:(hf + 1) * 128]
            cacc[hf, j] = half if fresh else cacc[hf, j] + half

    def q_pair(k):
        up, down = lax.rem(y + k, 8), lax.rem(y + 8 - k, 8)
        rows_up, rows_down = rows_of(up), rows_of(down)
        for j in range(4):
            lanes = pl.ds(j * 256, 256)
            q_add(j, dot(rows_up, qg[up, :, lanes]) + dot(rows_down, qg[down, :, lanes]))

    arrived(hx.at[1 - zl], h_sem)
    arrived(dtb.at[y, pl.ds(pl.multiple_of((1 - zl) * 8, 8), 8)], dt_sem)
    dt_ring.start()
    other_target = tgt_any.at[:, column(((1 - zl) * 8 + s) * 4 + q)]
    send(other_target, tg.at[zl], t_sem, flip_zl)
    rows = rows_of(y)
    for j in range(4):
        q_add(j, dot(rows, qg[y, :, pl.ds(j * 256, 256)]), True)
    q_ring.step(1, [0])
    kv_ring.step(2)
    q_ring.step(1, [1])
    hz_sem = sems(3)
    own_tile = hg.at[c, lax.div(tn, 2)]
    arrived(own_tile, p_sem)
    for d in range(1, 4):
        send(own_tile, own_tile, hz_sem + d - 1, zh_dev(d))
    q_pair(1)
    dt_ring.step(0)
    out_in.wait()
    q_ring.step(2, [0])
    kv_ring.step(3)
    k1_sem, k2_sem, k3_sem, k4_sem = sems(), sems(3), sems(7), sems()
    rows = jnp.concatenate([hx[0], hx[1]], axis=0)
    kvacc[...] = dot(rows, kvg[...].reshape(1024, 256))
    for zz in range(2):
        kvp[zz] = kvacc[pl.ds(pl.multiple_of(zz * 128 + (1 - c) * 64, 64), 64), :].astype(BF16)
    send(kvp, kvr1, k1_sem, flip_c)
    q_ring.step(2, [1])
    o_ring.start()
    dt_ring.step(1)
    arrived(kvr1, k1_sem)
    for zz in range(2):
        part = kvacc[pl.ds(pl.multiple_of(zz * 128 + c * 64, 64), 64), :] + kvr1[zz].astype(F32)
        kvt[zz] = part
        kvs[zz] = part.astype(BF16)
    send(kvs.at[1 - zl], kvr2.at[2], k2_sem + 2, flip_zh)
    send(kvs.at[zl], kvr2.at[0], k2_sem, flip_h)
    send(kvs.at[1 - zl], kvr2.at[1], k2_sem + 1, flip_zl)
    hx_sem = sems(3)
    for d in range(1, 4):
        arrived(hg.at[c, x * 4 + lax.rem(zh + 4 - d, 4)], hz_sem + d - 1)
    quad = hg.at[c, pl.ds(x * 4, 4)]
    for d in range(1, 4):
        send(quad, quad, hx_sem + d - 1, x_dev(d))
    q_pair(2)
    dt_ring.step(2)
    q_ring.step(3)
    for j in range(3):
        arrived(kvr2.at[j], k2_sem + j)
    kvall[c, s] = (
        kvt[zl] + kvr2[0].astype(F32) + kvr2[1].astype(F32) + kvr2[2].astype(F32)
    ).astype(BF16)
    own_kv = kvall.at[c, s]
    for d in (1, 3, 5, 7, 2, 4, 6):
        send(own_kv, own_kv, k3_sem + d - 1, s_dev(lax.rem(s + d, 8)))

    class Sum8:
        def __init__(self, acc, p1, r1, p2, r2, rows):
            self.acc, self.p1, self.r1, self.p2, self.r2 = acc, p1, r1, p2, r2
            self.rows = rows
            self.s1, self.s2 = sems(), sems(3)

        def first(self, add, fresh=False):
            n = self.rows
            for hh in range(2):
                part = add(hh * 2 + 1 - c)
                if not fresh:
                    part += self.acc[hh * 2 + 1 - c]
                for zz in range(2):
                    self.p1[zz, hh] = part[zz * n:(zz + 1) * n].astype(BF16)
            send(self.p1, self.r1, self.s1, flip_c)
            for hh in range(2):
                if fresh:
                    self.acc[hh * 2 + c] = add(hh * 2 + c)
                else:
                    self.acc[hh * 2 + c] += add(hh * 2 + c)

        def second(self):
            n = self.rows
            arrived(self.r1, self.s1)
            for zz in range(2):
                for hh in range(2):
                    rows = pl.ds(zz * n, n)
                    part = self.acc[hh * 2 + c, rows, :] + self.r1[zz, hh].astype(F32)
                    self.acc[hh * 2 + c, rows, :] = part
                    self.p2[zz, hh] = part.astype(BF16)
            send(self.p2.at[1 - zl, 1 - zh0], self.r2.at[2], self.s2 + 2, flip_zh)
            send(self.p2.at[zl, 1 - zh0], self.r2.at[0], self.s2, flip_h)
            send(self.p2.at[1 - zl, zh0], self.r2.at[1], self.s2 + 1, flip_zl)

        def third(self):
            n = self.rows
            for j in range(3):
                arrived(self.r2.at[j], self.s2 + j)
            own = self.acc[zh0 * 2 + c, pl.ds(pl.multiple_of(zl * n, n), n), :]
            return own + self.r2[0].astype(F32) + self.r2[1].astype(F32) + self.r2[2].astype(F32)

    c_sums = [
        Sum8(cacc.at[hf], cp1.at[hf], cr1.at[hf], cp2.at[hf], cr2.at[hf], 64) for hf in range(2)
    ]

    last = [lax.rem(y + k, 8) for k in (3, 4, 5)]
    last_rows = [rows_of(i) for i in last]
    for hf in range(2):

        def last_q(k):
            lanes = pl.ds(pl.multiple_of(k * 256, 256), 256)
            rows = slice(hf * 128, (hf + 1) * 128)
            return sum(dot(r[rows], qg[i, :, lanes]) for r, i in zip(last_rows, last))

        c_sums[hf].first(last_q)
    o_ring.step(0, [0])
    c_sums[0].second()
    c_sums[1].second()
    dt_ring.step(3)
    o_ring.step(0, [1])
    w2[...] = jnp.zeros_like(w2)
    for m in range(16):
        for j in range(4):
            for h in range(2):
                w2[h:h + 1, pl.ds((m * 4 + j) * 128, 128)] = dtb[
                    m % 8, pl.ds((m // 8) * 8 + h * 4 + j, 1), :
                ]

    o_ring.step(1, [0])
    best = dict(precision=lax.Precision.HIGHEST)
    weights = w2[...].astype(BF16)

    def softplus(v):
        return jnp.maximum(v, 0.0) + jnp.log1p(jnp.exp(-jnp.abs(v)))

    step_col = softplus(dot_t(hid[...], weights))
    step_row = softplus(dot_t(weights, hid[...]))
    dtc[...] = step_col
    rate0, rate1 = rate_ref[0], rate_ref[1]
    n_lane = step_col.shape[1]
    lane = lax.broadcasted_iota(jnp.int32, (TOK, n_lane), 1)
    subl = lax.broadcasted_iota(jnp.int32, (n_lane, TOK), 0)
    at_t = lax.broadcasted_iota(jnp.int32, (TOK, TOK), 0)
    at_j = lax.broadcasted_iota(jnp.int32, (TOK, TOK), 1)
    lower = (at_j <= at_t).astype(F32)
    upper = (at_t <= at_j).astype(F32)
    cs_col = dot(lower, step_col * jnp.where(lane == 0, rate0, rate1), **best)
    cs_row = dot(step_row * jnp.where(subl == 0, rate0, rate1), upper, **best)
    seg_row = jnp.broadcast_to(seg_ref[...].astype(F32), (TOK, TOK))
    visible = (seg_row == seg_row.T) & (at_j <= at_t)
    for h in range(2):
        distance = jnp.where(visible, cs_col[:, h:h + 1] - cs_row[h:h + 1, :], 0.0)
        mix[h] = jnp.where(visible, jnp.exp(-distance), 0.0)

    o_ring.step(1, [1])
    for d in range(1, 8):
        arrived(kvall.at[c, lax.rem(s + 8 - d, 8)], k3_sem + d - 1)
    send(kvall.at[c], kvall.at[c], k4_sem, flip_c)
    y_sem, y2_sem = sems(6), sems(2)
    arrived(kvall.at[1 - c], k4_sem)
    keys, sources = [], []
    for h in range(2):
        head = map_ref[h]
        both = jnp.concatenate([kvall[0, head], kvall[1, head]], axis=0)
        keys.append(both[:, :128])
        sources.append(dtc[:, h:h + 1] * both[:, 128:].astype(F32))

    def y_rows(hf, zz, hh):
        return yb.at[c, zz, hh, pl.ds(hf * 64, 64)]

    for hf in range(2):
        rows = pl.ds(hf * 64, 64)
        c_half = (c_sums[hf].third() * (128 ** -0.5)).astype(BF16)
        for h in range(2):
            lanes = slice(h * 128, (h + 1) * 128)
            mixing = dot_t(c_half[:, lanes], keys[h]) * mix[h, rows]
            mix[h, rows] = mixing
            yb[c, zl, zh0, rows, pl.ds(h * 128, 128)] = dot(
                mixing, sources[h], **best
            ).astype(BF16)
        own_y = y_rows(hf, zl, zh0)
        send(own_y, own_y, y_sem + hf * 3 + 2, flip_zh)
        send(own_y, own_y, y_sem + hf * 3, flip_h)
        send(own_y, own_y, y_sem + hf * 3 + 1, flip_zl)
    for h in range(2):
        mix[h] = mix[h].T
    o_ring.step(2)
    for hf in range(2):
        arrived(y_rows(hf, zl, 1 - zh0), y_sem + hf * 3)
        arrived(y_rows(hf, 1 - zl, zh0), y_sem + hf * 3 + 1)
        arrived(y_rows(hf, 1 - zl, 1 - zh0), y_sem + hf * 3 + 2)
        both_y = yb.at[c, :, :, pl.ds(hf * 64, 64)]
        send(both_y, both_y, y2_sem + hf, flip_c)
    hc_sem = sems()
    o_ring.step(3)

    def y_all(hf):
        arrived(yb.at[1 - c, :, :, pl.ds(hf * 64, 64)], y2_sem + hf)
        for zz in range(2):
            for hh in range(2):
                for cc in range(2):
                    rows = pl.ds(hf * 128 + zz * 64, 64)
                    lanes = pl.ds((hh * 2 + cc) * 256, 256)
                    ycat[rows, lanes] = yb[cc, zz, hh, pl.ds(hf * 64, 64)]

    halves = range(2)
    l0_sem, l1_sem, l2_sem = sems(6), sems(6), sems(2)
    for hf in halves:
        y_all(hf)
        for d in (2, 1, 3, 0):
            at = lax.rem(x + d, 4)
            lanes = pl.ds(pl.multiple_of(at * 256, 256), 256)
            value = dot(ycat[pl.ds(hf * 128, 128), :], og[:, lanes])
            if d:
                i = hf * 3 + d - 1
                lp[hf, at, 0] = value[:, :128].astype(BF16)
                lp[hf, at, 1] = value[:, 128:].astype(BF16)
                send(lp.at[hf, at, 1 - zh1], lr1.at[hf, 1, d - 1], l0_sem + i, x_dev(d))
            else:
                lt[hf, 0] = value[:, :128]
                lt[hf, 1] = value[:, 128:]
    for hf in halves:
        for d in (2, 1, 3):
            at = lax.rem(x + d, 4)
            send(lp.at[hf, at, zh1], lr1.at[hf, 0, d - 1], l1_sem + hf * 3 + d - 1, x_dev(d))
    for hf in halves:
        part = lt[hf, 1 - zh1]
        for d in range(3):
            arrived(lr1.at[hf, 1, d], l0_sem + hf * 3 + d)
            part += lr1[hf, 1, d].astype(F32)
        ls[hf] = part.astype(BF16)
        send(ls.at[hf], lr2.at[hf], l2_sem + hf, flip_h1)
    for d in range(1, 4):
        arrived(hg.at[c, pl.ds(lax.rem(x + 4 - d, 4) * 4, 4)], hx_sem + d - 1)
    send(hg.at[c], hg.at[c], hc_sem, flip_c)
    target_in.wait()
    arrived(tg.at[1 - zl], t_sem)
    g1_sem, g2_sem, g3_sem, la_sem, la2_sem = sems(2), sems(6), sems(6), sems(), sems(3)
    squares = jnp.zeros((8, 128), F32)

    def g_piece(hf, index):
        return gob.at[pl.ds(hf * 128, 128), column(index)]

    for hf in halves:
        part = lt[hf, zh1]
        for d in range(3):
            arrived(lr1.at[hf, 0, d], l1_sem + hf * 3 + d)
            part += lr1[hf, 0, d].astype(F32)
        arrived(lr2.at[hf], l2_sem + hf)
        layer = (part + lr2[hf].astype(F32)).astype(BF16)
        for zz in range(2):
            rows = layer[zz * 64:(zz + 1) * 64]
            lob[zz, pl.ds(hf * 64, 64)] = rows
            residual = rows.astype(F32) - tg[zz, pl.ds(hf * 64, 64)].astype(F32)
            gob[pl.ds(hf * 128 + zz * 64, 64), column(s)] = (2.0 * residual / TOKENS).astype(BF16)
            squares += jnp.sum((residual * residual).reshape(8, 8, 128), axis=0)
        own_g = g_piece(hf, s)
        send(own_g, own_g, g1_sem + hf, flip_h1)
        for d in (2, 1, 3):
            send(own_g, own_g, g2_sem + hf * 3 + d - 1, x_dev(d))
    lsa[s] = squares
    send(lsa.at[s], lsa.at[s], la_sem, flip_h1)
    for hf in halves:
        next_g = g_piece(hf, 2 * x + 1 - zh1)
        arrived(next_g, g1_sem + hf)
        for d in (2, 1, 3):
            send(next_g, next_g, g3_sem + hf * 3 + d - 1, x_dev(d))

    lo_sem = sems(2)
    lo_tn = 16 * zl + 2 * s + lax.div(q, 2)
    slot = lax.rem(q, 2)
    lo_dst = lo_ref.at[:, column(slot)]
    lo_copies = []
    for zz in range(2):
        to = (zz * 8 + y, lo_tn)
        here = (zl == zz) & (lo_tn == tn)
        copy = pltpu.make_async_remote_copy(
            src_ref=lob.at[zz], dst_ref=lo_dst, send_sem=ssem.at[lo_sem + zz],
            recv_sem=rsem.at[lo_sem + slot], device_id=to, device_id_type=MESH,
        )
        lo_copies.append((copy, here))

        @pl.when(here)
        def _():
            lo_ref[:, column(slot)] = lob[zz]

        @pl.when(jnp.logical_not(here))
        def _():
            copy.start()

    arrived(lsa.at[2 * x + 1 - zh1], la_sem)
    loss_pair = lsa.at[pl.ds(x * 2, 2)]
    for d in range(1, 4):
        send(loss_pair, loss_pair, la2_sem + d - 1, x_dev(d))
    d_sums = [
        Sum8(dacc.at[hf], dp1.at[hf], dr1.at[hf], dp2.at[hf], dr2.at[hf], 64) for hf in halves
    ]
    for hf in halves:
        for d in (1, 3, 2):
            at = lax.rem(x + 4 - d, 4)
            arrived(g_piece(hf, at * 2 + zh1), g2_sem + hf * 3 + d - 1)
            arrived(g_piece(hf, at * 2 + 1 - zh1), g3_sem + hf * 3 + d - 1)
        rows = gob[pl.ds(hf * 128, 128), :]

        def part(k):
            return dot_t(rows, og[pl.ds(pl.multiple_of(k * 256, 256), 256), :])

        d_sums[hf].first(part, True)
        if hf:
            d_sums[0].second()
    d_sums[1].second()
    lb_sem, lc_sem = sems(), sems(3)
    for d in range(1, 4):
        arrived(lsa.at[pl.ds(lax.rem(x + 4 - d, 4) * 2, 2)], la2_sem + d - 1)
    total = lsa[0]
    for i in range(1, 8):
        total += lsa[i]
    lsb[...] = total
    send(lsb, lsb1, lb_sem, flip_c)
    arrived(lsb1, lb_sem)
    lsc[...] = lsb[...] + lsb1[...]
    for j in range(3):
        send(lsc, lsc2.at[j], lc_sem + j, line[j])
    dy = jnp.concatenate([d_sums[hf].third() for hf in halves], axis=0)
    dy = dy.astype(BF16).astype(F32)
    dx_sem = sems()
    for h in range(2):
        back = dot(mix[h], dy[:, h * 128:(h + 1) * 128], **best)
        dxb[y, zl, :, pl.ds(h * 128, 128)] = (dtc[:, h:h + 1] * back).astype(BF16)
    send(dxb.at[y, zl], dxb.at[y, zl], dx_sem, flip_zl)
    dx_ring.start([0])
    for j in range(3):
        arrived(lsc2.at[j], lc_sem + j)
    lring[y] = lsc[...] + lsc2[0] + lsc2[1] + lsc2[2]
    arrived(dxb.at[y, 1 - zl], dx_sem)
    dx_ring.start([1])
    loss_ring.start()
    arrived(hg.at[1 - c], hc_sem)

    def g_block(i, first=False):
        grads = jnp.concatenate([dxb[i, 0], dxb[i, 1]], axis=0)
        for b in range(2):
            tokens = jnp.concatenate([hg[b, 8 + i], hg[b, i]], axis=1)
            rows = pl.ds(b * 256, 256)
            if first:
                gx_ref[rows, :] = dot(tokens, grads)
            else:
                gx_ref[rows, :] += dot(tokens, grads)

    g_block(y, True)
    for k in range(4):
        dx_ring.step(k)
        loss_ring.step(k)
        g_block(lax.rem(y + 7 - k, 8))
        if k < 3:
            g_block(lax.rem(y + k + 1, 8))
    total = jnp.sum(jnp.sum(lring[...], axis=0), axis=0, keepdims=True)
    total = jnp.sum(total, axis=1, keepdims=True) / (TOKENS * WIDTH)
    loss_ref[...] = total

    for copy in pending:
        copy.wait_send()
    for copy, here in lo_copies:
        @pl.when(jnp.logical_not(here))
        def _():
            copy.wait_send()
    for k in range(2):
        from_dp, from_tn = lo_source(k)
        here = (from_dp == dp) & (from_tn == tn)

        @pl.when(jnp.logical_not(here))
        def _():
            arrived(lo_ref.at[:, pl.ds(k * 128, 128)], lo_sem + k)


def store(lo_in, gx_in, loss_in, lo_out, gx_out, loss_out, lo, gx, loss, sem):
    trips = ((gx_in, gx, gx_out), (lo_in, lo, lo_out), (loss_in, loss, loss_out))
    reads = [pltpu.make_async_copy(a, b, sem.at[i]) for i, (a, b, _) in enumerate(trips)]
    writes = [pltpu.make_async_copy(b, d, sem.at[3 + i]) for i, (_, b, d) in enumerate(trips)]
    for move in reads:
        move.start()
    for read, write in zip(reads, writes):
        read.wait()
        write.start()
    for move in writes:
        move.wait()


def local(
    hidden, target, segments, head_map, decay_rate, dt_weight,
    teacher_query, teacher_key, teacher_value, teacher_out,
):
    steps = dt_weight.T
    anywhere = pl.BlockSpec(memory_space=pltpu.HBM)
    vmem = pl.BlockSpec(memory_space=pltpu.VMEM)
    smem = pl.BlockSpec(memory_space=pltpu.SMEM)

    def b(*shape):
        return pltpu.VMEM(shape, BF16)

    def f(*shape):
        return pltpu.VMEM(shape, F32)

    scratch = [
        b(128, 8192), b(2, 128, 128), b(8, 128, 1024), b(8, 128, 256), b(1024, 1024),
        f(8, 16, 128), b(2, 128, 1024), b(128, 1024), b(256, 128), b(2, 16, 256, 128),
        f(256, 256), b(2, 64, 256), b(2, 64, 256), f(2, 64, 256), b(2, 64, 256), b(3, 64, 256),
        b(2, 8, 64, 256),
        f(2, 4, 128, 256), b(2, 2, 2, 64, 256), b(2, 2, 2, 64, 256), b(2, 2, 2, 64, 256),
        b(2, 3, 64, 256),
        f(16, 8192), f(2, 128, 128), f(128, 16), b(2, 2, 2, 128, 256), b(256, 1024),
        b(2, 4, 2, 128, 128), b(2, 2, 3, 128, 128), f(2, 2, 128, 128), b(2, 128, 128),
        b(2, 128, 128), b(2, 128, 128),
        b(256, 1024), f(2, 4, 128, 256), b(2, 2, 2, 64, 256), b(2, 2, 2, 64, 256),
        b(2, 2, 2, 64, 256), b(2, 3, 64, 256), b(8, 2, 128, 256),
        f(8, 8, 128), f(8, 128), f(8, 128), f(8, 128), f(3, 8, 128), f(8, 8, 128),
        pltpu.SemaphoreType.DMA((N_SEM,)), pltpu.SemaphoreType.DMA((N_SEM,)),
        pltpu.SemaphoreType.DMA((6,)),
    ]
    layer_out, grad_x, loss = pl.pallas_call(
        kernel,
        out_shape=(
            jax.ShapeDtypeStruct((128, 256), BF16),
            jax.ShapeDtypeStruct((512, 256), F32),
            jax.ShapeDtypeStruct((1, 1), F32),
        ),
        in_specs=[anywhere, anywhere, vmem, smem, smem, vmem] + [anywhere] * 4,
        out_specs=(vmem, vmem, vmem),
        scratch_shapes=scratch,
        compiler_params=pltpu.CompilerParams(
            collective_id=0, has_side_effects=True, vmem_limit_bytes=65536 * 1024 - 640 * 1024
        ),
    )(
        hidden, target, segments, head_map, decay_rate, steps,
        teacher_query[0], teacher_key[0], teacher_value[0], teacher_out[0],
    )
    layer_out, grad_x, loss = pl.pallas_call(
        store,
        out_shape=(
            jax.ShapeDtypeStruct((128, 256), BF16),
            jax.ShapeDtypeStruct((512, 256), F32),
            jax.ShapeDtypeStruct((1, 1), F32),
        ),
        in_specs=[anywhere] * 3,
        out_specs=(anywhere,) * 3,
        scratch_shapes=[
            b(128, 256), f(512, 256), f(1, 1), pltpu.SemaphoreType.DMA((6,)),
        ],
    )(layer_out, grad_x, loss)
    return layer_out, grad_x, loss[0, 0]


def solution(mesh):
    in_specs = (
        P("dp", None),
        P("dp", None),
        P("dp", None),
        P("tensor"),
        P("tensor"),
        P("dp", "tensor"),
        P("tensor", "dp", None),
        P("tensor", "dp", None),
        P("tensor", "dp", None),
        P("tensor", None, "dp"),
    )
    out_specs = (P("dp", "tensor"), P("dp", "tensor"), P())
    return jax.shard_map(local, mesh=mesh, in_specs=in_specs, out_specs=out_specs, check_vma=False)
```
